32 devices in a mesh: seq: 4 (over y, x), fsdp: 8 (over z, core).
Axes of the slice: x: 2, y: 2, z: 4, core: 2. Of those that a mesh axis runs over, the one named last changes fastest.
Arguments:
- token_ids: int32 [2, 8, 1024], P(None, 'fsdp', 'seq'), may hold values from 0 to 32127
- lengths: int32 [2, 8], P(None, 'fsdp'), may hold values from 683 to 1024, as said below
- routes: int32 [2, 8, 1024, 1], P(None, 'fsdp', 'seq'), may hold values from 0 to 3; in each aligned block of 256 rows (0 to 255, 256 to 511, ..., all dimensions but the last counted through in order) at most 96 rows name the same one
- positions: int32 [2, 8, 128], P(None, 'fsdp', 'seq'), may hold values from 0 to 255
- targets: int32 [2, 8, 128], P(None, 'fsdp', 'seq'), may hold values from 0 to 32127
- teacher_index: int32 [2, 8, 128, 64], P(None, 'fsdp', 'seq'), may hold values from 0 to 32127, as said below
- teacher_weight: float32 [2, 8, 128, 64], P(None, 'fsdp', 'seq'), may hold values from 0.001 to 1
- buckets: int32 [2047], replicated, may hold values from 0 to 31
- embed_weight: float32 [32128, 768], P('fsdp'), may hold values from -6 to 6
- embed_mean: float32 [32128, 768], P('fsdp'), may hold values from -7.6293945e-05 to 7.6293945e-05
- embed_square: float32 [32128, 768], P('fsdp'), may hold values from 1.4891505e-11 to 5.956602e-11
- attend_weight: float32 [2, 768, 2304], P(None, 'fsdp'), may hold values from -0.21875 to 0.21875
- attend_mean: float32 [2, 768, 2304], P(None, 'fsdp'), may hold values from -7.6293945e-05 to 7.6293945e-05
- attend_square: float32 [2, 768, 2304], P(None, 'fsdp'), may hold values from 1.4891505e-11 to 5.956602e-11
- output_weight: float32 [2, 768, 768], P(None, 'fsdp'), may hold values from -2.5 to 2.5
- output_mean: float32 [2, 768, 768], P(None, 'fsdp'), may hold values from -7.6293945e-05 to 7.6293945e-05
- output_square: float32 [2, 768, 768], P(None, 'fsdp'), may hold values from 1.4891505e-11 to 5.956602e-11
- upward_weight: float32 [2, 4, 768, 3072], P(None, None, 'fsdp'), may hold values from -0.21875 to 0.21875
- upward_mean: float32 [2, 4, 768, 3072], P(None, None, 'fsdp'), may hold values from -7.6293945e-05 to 7.6293945e-05
- upward_square: float32 [2, 4, 768, 3072], P(None, None, 'fsdp'), may hold values from 3.722876e-12 to 1.4891505e-11
- downward_weight: float32 [2, 4, 3072, 768], P(None, None, 'fsdp'), may hold values from -0.3125 to 0.3125
- downward_mean: float32 [2, 4, 3072, 768], P(None, None, 'fsdp'), may hold values from -7.6293945e-05 to 7.6293945e-05
- downward_square: float32 [2, 4, 3072, 768], P(None, None, 'fsdp'), may hold values from 3.722876e-12 to 1.4891505e-11
- router_weight: float32 [2, 768, 4], P(None, 'fsdp'), may hold values from -0.15625 to 0.15625
- router_mean: float32 [2, 768, 4], P(None, 'fsdp'), may hold values from -7.6293945e-05 to 7.6293945e-05
- router_square: float32 [2, 768, 4], P(None, 'fsdp'), may hold values from 1.4891505e-11 to 5.956602e-11
- gains_weight: float32 [5, 768], P(None, 'fsdp'), may hold values from 0.5 to 1.5
- gains_mean: float32 [5, 768], P(None, 'fsdp'), may hold values from -7.6293945e-05 to 7.6293945e-05
- gains_square: float32 [5, 768], P(None, 'fsdp'), may hold values from 1.4891504e-09 to 5.9566014e-09
- bias_weight: float32 [2, 384], P(None, 'fsdp'), may hold values from -6 to 6
- bias_mean: float32 [2, 384], P(None, 'fsdp'), may hold values from -7.6293945e-05 to 7.6293945e-05
- bias_square: float32 [2, 384], P(None, 'fsdp'), may hold values from 1.4891505e-11 to 5.956602e-11
Outputs:
- loss_sum: float32 [], replicated
- loss_count: float32 [], replicated
- grad_norm: float32 [], replicated
- embed_weight_next: float32 [32128, 768], P('fsdp')
- embed_mean_next: float32 [32128, 768], P('fsdp')
- embed_square_next: float32 [32128, 768], P('fsdp')
- attend_weight_next: float32 [2, 768, 2304], P(None, 'fsdp')
- attend_mean_next: float32 [2, 768, 2304], P(None, 'fsdp')
- attend_square_next: float32 [2, 768, 2304], P(None, 'fsdp')
- output_weight_next: float32 [2, 768, 768], P(None, 'fsdp')
- output_mean_next: float32 [2, 768, 768], P(None, 'fsdp')
- output_square_next: float32 [2, 768, 768], P(None, 'fsdp')
- upward_weight_next: float32 [2, 4, 768, 3072], P(None, None, 'fsdp')
- upward_mean_next: float32 [2, 4, 768, 3072], P(None, None, 'fsdp')
- upward_square_next: float32 [2, 4, 768, 3072], P(None, None, 'fsdp')
- downward_weight_next: float32 [2, 4, 3072, 768], P(None, None, 'fsdp')
- downward_mean_next: float32 [2, 4, 3072, 768], P(None, None, 'fsdp')
- downward_square_next: float32 [2, 4, 3072, 768], P(None, None, 'fsdp')
- router_weight_next: float32 [2, 768, 4], P(None, 'fsdp')
- router_mean_next: float32 [2, 768, 4], P(None, 'fsdp')
- router_square_next: float32 [2, 768, 4], P(None, 'fsdp')
- gains_weight_next: float32 [5, 768], P(None, 'fsdp')
- gains_mean_next: float32 [5, 768], P(None, 'fsdp')
- gains_square_next: float32 [5, 768], P(None, 'fsdp')
- bias_weight_next: float32 [2, 384], P(None, 'fsdp')
- bias_mean_next: float32 [2, 384], P(None, 'fsdp')
- bias_square_next: float32 [2, 384], P(None, 'fsdp')
The draws below stay inside these ranges and needn't reach their ends.
Inputs may be any that keep to these rules, and one draw needn't show every extreme that they name: `lengths`: in every micro-batch one sequence has length 1024. `routes`: in every aligned block of 256 rows (the rows of one device) no expert is named more than 96 times. `positions`: entries j * 32 to j * 32 + 31 of a row index block j of 256 tokens. `teacher_index`: the 64 entries of a row differ.
All inputs are finite; a program needn't handle non-finite values.
Results may differ from the reference program's by a relative error of at most 0.018.
The reference program's roundings to bfloat16 on the way count: a program that leaves them out, or rounds other values in their place, can miss the bound.
Values may be sent and summed in bfloat16 or wider, within the bound.
No kernel may reach another device: no remote copies, remote signals or barrier semaphores. Data moves between devices by JAX's collectives and lax.ppermute only.
A program may use at most 1.125 GiB of HBM per device.

```python
import math
import jax
import jax.numpy as jnp
import numpy as np
from jax import lax

D = 768
H = 12
HD = 64
FF = 3072
V = 32128
EXPERTS = 4
LAYERS = 2
MB = 2
SEQ_DEV = 256
NPOS = 32
TOPT = 64
NB = 32
STEP_COUNT = 10
SEQ = 1024
BATCH = 8
CAP = 96
POSITIONS = 128
RELS = 2047
PARAMS = 67152384


def draw_lengths(key, part):
    key = jax.random.fold_in(key, 5)
    first_key, second_key = jax.random.split(key)
    base = jax.random.randint(first_key, (MB, BATCH), SEQ - SEQ // 3, SEQ + 1)
    longest = jax.random.randint(second_key, (MB,), 0, BATCH)
    chosen = jnp.arange(BATCH)[None, :] == longest[:, None]
    return jnp.where(chosen, SEQ, base).astype(jnp.int32)


def draw_teacher_index(key, part):
    key = jax.random.fold_in(key, 7)
    first_key, second_key = jax.random.split(key)
    stride = V // TOPT
    start = jax.random.randint(first_key, (MB, BATCH, POSITIONS, 1), 0, V)
    jitter = jax.random.randint(second_key, (MB, BATCH, POSITIONS, TOPT), 0, stride)
    spaced = jnp.arange(TOPT, dtype=jnp.int32)[None, None, None, :] * stride
    return ((start + spaced + jitter) % V).astype(jnp.int32)


def plant(result, stream_key, smallest, high):
    extent = result.shape
    index_at = [jax.random.randint(jax.random.fold_in(stream_key, axis), (), 0, extent[axis]) for axis in range(len(extent))]
    result = result.at[tuple(index_at)].set(smallest)
    longest = extent.index(max(extent))
    index_at[longest] = (index_at[longest] + 1) % extent[longest]
    return result.at[tuple(index_at)].set(high)


def steps_of(key, dims, cuts, low, largest):
    factor_of, own = 1.0, jax.random.fold_in(key, 6)
    for position, shards_of in cuts:
        steps = jnp.exp(jax.random.uniform(jax.random.fold_in(own, position), (shards_of,), jnp.float32, low / len(cuts), largest / len(cuts)))
        factor_of = factor_of * jnp.repeat(steps, dims[position] // shards_of).reshape([-1 if axis == position else 1 for axis in range(len(dims))])
    return factor_of


def rank_bounds(number_of, slope):
    weights = [(1 << 20) // math.isqrt(rank ** slope) + 1 for rank in range(1, number_of + 1)]
    scale = 1 + sum(weights) // (1 << 30)
    return np.cumsum(np.array([max(1, weight // scale) for weight in weights]))


def ranked_ids(own_key, shape, count, lean):
    table = rank_bounds(count, lean)
    lot = jax.random.randint(jax.random.fold_in(own_key, 1), shape, 0, int(table[count - 1]))
    rank = jnp.searchsorted(jnp.asarray(table, jnp.int32), lot, side="right")
    return jax.random.permutation(jax.random.fold_in(own_key, 2), count)[rank].astype(jnp.int32)


def shared_out(key, own, number, rows, count, top, reach, lean):
    sequence = jax.random.permutation(key, count)
    heavy_load, common = load_shares(count, rows * top, reach, lean, True), load_shares(count, rows * top, reach, lean, False)
    places = jnp.arange(count)

    def named(sizes, turn):
        used = int((sizes > 0).sum())
        fixed = max(1, used // 4)
        shifted = fixed + (places - fixed + turn * (used - fixed)) % max(1, count - fixed)
        return jnp.zeros((count,), jnp.int32).at[sequence[jnp.where(places < fixed, places, shifted)]].set(jnp.asarray(sizes, jnp.int32))

    sizes = jnp.where(number % 4 == 0, named(heavy_load, number // 4), named(common, number - number // 4 - 1))
    mixed = jax.random.permutation(jax.random.fold_in(own, 3), count)
    giver, receiver = mixed[0:count // 2 * 2:2], mixed[1:count // 2 * 2:2]
    margin = jnp.minimum(sizes[giver] - 1, reach - sizes[receiver]) // 2
    margin = jnp.where((giver == sequence[0]) | (receiver == sequence[0]) | (sizes[receiver] == 0), 0, jnp.maximum(margin, 0))
    shifted = jax.random.randint(jax.random.fold_in(own, 4), (count // 2,), 0, 1 << 20) % (margin + 1)
    sizes = sizes.at[giver].add(-shifted).at[receiver].add(shifted)
    members = jnp.searchsorted(jnp.cumsum(sizes), jnp.arange(rows * top), side="right").astype(jnp.int32)
    listing = members.reshape(top, rows).T
    listing = listing[jax.random.permutation(jax.random.fold_in(own, 1), rows)]
    turn = jax.random.randint(jax.random.fold_in(own, 2), (rows, 1), 0, top)
    return jnp.take_along_axis(listing, (jnp.arange(top)[None, :] + turn) % top, axis=1)


def load_shares(count, total, limit, slope, full):
    weights = [(1 << 20) // math.isqrt(rank ** slope) + 1 for rank in range(1, count + 1)]
    largest = limit if full else min(limit, max(-(-total // count), total * weights[0] // sum(weights)))
    least = 1 if total - largest >= count - 1 else 0
    holding, rest = [largest] + [least] * (count - 1), total - largest - least * (count - 1)
    while rest > 0:
        free = [i for i in range(1, count) if holding[i] < largest] or [i for i in range(1, count) if holding[i] < limit]
        mass, budget = sum([weights[i] for i in free]), rest
        for i in free:
            addition = min(limit - holding[i], max(1, budget * weights[i] // mass), rest)
            holding[i] = holding[i] + addition
            rest = rest - addition
    return np.array(holding)


def scatter_about(own_key, extent, spread, most, shards=(), kind=jnp.bfloat16):
    entries = jax.random.normal(own_key, extent, jnp.float32) * spread
    if len(shards) > 0:
        entries = steps_of(own_key, extent, shards, -0.22, 0.18) * entries
    return jnp.clip(entries, min=-most, max=most).astype(kind)


def setup_inputs(seed: int = 0) -> dict:
    arg_keys = jax.random.split(jax.random.key(seed), 33)
    token_ids = plant(ranked_ids(arg_keys[0], (MB, BATCH, SEQ), V, 2), jax.random.fold_in(arg_keys[0], 3), 0, V - 1).astype(jnp.int32)
    lengths = draw_lengths(jax.random.fold_in(arg_keys[32], 71), 0)
    routes_keys = jax.random.split(jax.random.fold_in(arg_keys[2], 1), MB * BATCH * SEQ // SEQ_DEV)
    routes_turns = jax.random.permutation(jax.random.fold_in(arg_keys[2], 3), MB * BATCH * SEQ // SEQ_DEV)
    routes = jax.vmap(lambda own, number: shared_out(jax.random.fold_in(arg_keys[2], 2), own, number, SEQ_DEV, EXPERTS, 1, CAP, 2))(routes_keys, routes_turns).reshape((MB, BATCH, SEQ, 1))
    positions = plant(jax.random.randint(arg_keys[3], (MB, BATCH, POSITIONS), 0, SEQ_DEV), jax.random.fold_in(arg_keys[3], 1), 0, SEQ_DEV - 1).astype(jnp.int32)
    targets = plant(ranked_ids(arg_keys[4], (MB, BATCH, POSITIONS), V, 2), jax.random.fold_in(arg_keys[4], 3), 0, V - 1).astype(jnp.int32)
    teacher_index = draw_teacher_index(jax.random.fold_in(arg_keys[32], 71), 0)
    teacher_weight = jnp.clip(jnp.exp(math.log(1.0) - 6.9077552 * jax.random.uniform(arg_keys[6], (MB, BATCH, POSITIONS, TOPT), jnp.float32) ** steps_of(arg_keys[6], (MB, BATCH, POSITIONS, TOPT), ((1, 8), (2, 4)), -0.2, 0.2)), 0.001, 1.0)
    buckets = plant(jax.random.randint(arg_keys[7], (RELS,), 0, NB), jax.random.fold_in(arg_keys[7], 1), 0, NB - 1).astype(jnp.int32)
    embed_weight = scatter_about(arg_keys[8], (V, D), 1.0, 6.0, ((0, 8),), jnp.float32)
    embed_mean = scatter_about(arg_keys[9], (V, D), (0.11 * PARAMS ** -0.5), 7.62939453125e-05, ((0, 8),), jnp.float32)
    embed_square = jnp.clip(jnp.exp(math.log(5.956601878409629e-11) - 1.3862944 * jax.random.uniform(arg_keys[10], (V, D), jnp.float32) ** steps_of(arg_keys[10], (V, D), ((0, 8),), -0.2, 0.2)), 1.489150469602407e-11, 5.956601878409629e-11)
    attend_weight = scatter_about(arg_keys[11], (LAYERS, D, 3 * D), D ** -0.5, 0.21875, ((1, 8),), jnp.float32)
    attend_mean = scatter_about(arg_keys[12], (LAYERS, D, 3 * D), (0.11 * PARAMS ** -0.5), 7.62939453125e-05, ((1, 8),), jnp.float32)
    attend_square = jnp.clip(jnp.exp(math.log(5.956601878409629e-11) - 1.3862944 * jax.random.uniform(arg_keys[13], (LAYERS, D, 3 * D), jnp.float32) ** steps_of(arg_keys[13], (LAYERS, D, 3 * D), ((1, 8),), -0.2, 0.2)), 1.489150469602407e-11, 5.956601878409629e-11)
    output_weight = scatter_about(arg_keys[14], (LAYERS, D, D), (max(D * 8 // SEQ, 1)) ** -0.5, 2.5, ((1, 8),), jnp.float32)
    output_mean = scatter_about(arg_keys[15], (LAYERS, D, D), (0.11 * PARAMS ** -0.5), 7.62939453125e-05, ((1, 8),), jnp.float32)
    output_square = jnp.clip(jnp.exp(math.log(5.956601878409629e-11) - 1.3862944 * jax.random.uniform(arg_keys[16], (LAYERS, D, D), jnp.float32) ** steps_of(arg_keys[16], (LAYERS, D, D), ((1, 8),), -0.2, 0.2)), 1.489150469602407e-11, 5.956601878409629e-11)
    upward_weight = scatter_about(arg_keys[17], (LAYERS, EXPERTS, D, FF), D ** -0.5, 0.21875, ((2, 8),), jnp.float32)
    upward_mean = scatter_about(arg_keys[18], (LAYERS, EXPERTS, D, FF), (0.11 * PARAMS ** -0.5), 7.62939453125e-05, ((2, 8),), jnp.float32)
    upward_square = jnp.clip(jnp.exp(math.log(1.489150469602407e-11) - 1.3862944 * jax.random.uniform(arg_keys[19], (LAYERS, EXPERTS, D, FF), jnp.float32) ** steps_of(arg_keys[19], (LAYERS, EXPERTS, D, FF), ((2, 8),), -0.2, 0.2)), 3.722876174006018e-12, 1.489150469602407e-11)
    downward_weight = scatter_about(arg_keys[20], (LAYERS, EXPERTS, FF, D), (FF // 8) ** -0.5, 0.3125, ((2, 8),), jnp.float32)
    downward_mean = scatter_about(arg_keys[21], (LAYERS, EXPERTS, FF, D), (0.11 * PARAMS ** -0.5), 7.62939453125e-05, ((2, 8),), jnp.float32)
    downward_square = jnp.clip(jnp.exp(math.log(1.489150469602407e-11) - 1.3862944 * jax.random.uniform(arg_keys[22], (LAYERS, EXPERTS, FF, D), jnp.float32) ** steps_of(arg_keys[22], (LAYERS, EXPERTS, FF, D), ((2, 8),), -0.2, 0.2)), 3.722876174006018e-12, 1.489150469602407e-11)
    router_weight = scatter_about(arg_keys[23], (LAYERS, D, EXPERTS), (2 * D) ** -0.5, 0.15625, ((1, 8),), jnp.float32)
    router_mean = scatter_about(arg_keys[24], (LAYERS, D, EXPERTS), (0.11 * PARAMS ** -0.5), 7.62939453125e-05, ((1, 8),), jnp.float32)
    router_square = jnp.clip(jnp.exp(math.log(5.956601878409629e-11) - 1.3862944 * jax.random.uniform(arg_keys[25], (LAYERS, D, EXPERTS), jnp.float32) ** steps_of(arg_keys[25], (LAYERS, D, EXPERTS), ((1, 8),), -0.2, 0.2)), 1.489150469602407e-11, 5.956601878409629e-11)
    gains_weight = jnp.clip(1.0 + 0.1 * jax.random.normal(arg_keys[26], (2 * LAYERS + 1, D), jnp.float32), 0.5, 1.5)
    gains_mean = scatter_about(arg_keys[27], (2 * LAYERS + 1, D), (0.11 * PARAMS ** -0.5), 7.62939453125e-05, ((1, 8),), jnp.float32)
    gains_square = jnp.clip(jnp.exp(math.log(5.956601434320419e-09) - 1.3862944 * jax.random.uniform(arg_keys[28], (2 * LAYERS + 1, D), jnp.float32) ** steps_of(arg_keys[28], (2 * LAYERS + 1, D), ((1, 8),), -0.2, 0.2)), 1.4891503585801047e-09, 5.956601434320419e-09)
    bias_weight = scatter_about(arg_keys[29], (LAYERS, NB * H), 1.0, 6.0, ((1, 8),), jnp.float32)
    bias_mean = scatter_about(arg_keys[30], (LAYERS, NB * H), (0.11 * PARAMS ** -0.5), 7.62939453125e-05, ((1, 8),), jnp.float32)
    bias_square = jnp.clip(jnp.exp(math.log(5.956601878409629e-11) - 1.3862944 * jax.random.uniform(arg_keys[31], (LAYERS, NB * H), jnp.float32) ** steps_of(arg_keys[31], (LAYERS, NB * H), ((1, 8),), -0.2, 0.2)), 1.489150469602407e-11, 5.956601878409629e-11)
    return {"token_ids": token_ids, "lengths": lengths, "routes": routes, "positions": positions, "targets": targets, "teacher_index": teacher_index, "teacher_weight": teacher_weight, "buckets": buckets, "embed_weight": embed_weight, "embed_mean": embed_mean, "embed_square": embed_square, "attend_weight": attend_weight, "attend_mean": attend_mean, "attend_square": attend_square, "output_weight": output_weight, "output_mean": output_mean, "output_square": output_square, "upward_weight": upward_weight, "upward_mean": upward_mean, "upward_square": upward_square, "downward_weight": downward_weight, "downward_mean": downward_mean, "downward_square": downward_square, "router_weight": router_weight, "router_mean": router_mean, "router_square": router_square, "gains_weight": gains_weight, "gains_mean": gains_mean, "gains_square": gains_square, "bias_weight": bias_weight, "bias_mean": bias_mean, "bias_square": bias_square}


@jax.custom_vjp
def low(v):
    return lax.optimization_barrier(v.astype(jnp.bfloat16)).astype(jnp.float32)

@jax.custom_vjp
def low_back(v):
    return v

def low_keep(v):
    return (low(v), None)

def low_pass(kept, grad):
    return (grad,)

def back_keep(v):
    return (v, None)

def back_low(kept, grad):
    return (low(grad),)
low.defvjp(low_keep, low_pass)
low_back.defvjp(back_keep, back_low)
EPSILON = 1e-06
ADAM_EPSILON = 1e-08
BETA_ONE = 0.9
BETA_TWO = 0.999
WEIGHT_DECAY = 0.01
CLIP_NORM = 1.0
STEP_RATES = (0.5, 0.03, 0.3, 0.03, 0.04, 0.02, 0.9, 0.5)
HIGHEST_PRECISION = lax.Precision.HIGHEST

def rms(hidden, gain):
    return hidden * lax.rsqrt(lax.optimization_barrier(jnp.mean(hidden * hidden, -1, keepdims=True)) + EPSILON) * gain

def attention(query_rows, key_rows, value_rows, seq_length, table, buckets):
    total_rows = query_rows.shape[0]
    query_h = query_rows.reshape(total_rows, H, HD)
    key_h = key_rows.reshape(total_rows, H, HD)
    value_h = value_rows.reshape(total_rows, H, HD)
    relative = table[buckets]
    row_ids = jnp.arange(total_rows)
    offsets = row_ids[None, :] - row_ids[:, None] + total_rows - 1
    bias = relative[offsets].transpose(2, 0, 1)
    scores = jnp.einsum('qhd,khd->hqk', query_h, key_h, precision=HIGHEST_PRECISION) * HD ** (-0.5) + bias
    scores = low_back(scores)
    scores = jnp.where((row_ids < seq_length)[None, None, :], scores, -1e+30)
    weights = low(jax.nn.softmax(scores, -1))
    return jnp.einsum('hqk,khd->qhd', weights, value_h, precision=HIGHEST_PRECISION).reshape(total_rows, -1)

def expert_block(rows, route_ids, upward, downward):
    onehot = (route_ids[:, None] == jnp.arange(EXPERTS)[None, :]).astype(jnp.float32)
    slot_ranks = lax.optimization_barrier(jnp.sum((jnp.cumsum(onehot, 0) - 1.0) * onehot, -1)).astype(jnp.int32)
    slot_index = route_ids * CAP + slot_ranks
    dispatch = (slot_index[None, :] == jnp.arange(EXPERTS * CAP)[:, None]).astype(jnp.float32)
    expert_rows = jnp.dot(dispatch, rows, precision=HIGHEST_PRECISION, preferred_element_type=jnp.float32).reshape(EXPERTS, CAP, D)
    upward_val = low_back(jnp.einsum('ecd,edf->ecf', expert_rows, upward, precision=HIGHEST_PRECISION))
    activated = low(jax.nn.gelu(upward_val))
    expert_out = jnp.einsum('ecf,efd->ecd', activated, downward, precision=HIGHEST_PRECISION).reshape(EXPERTS * CAP, D)
    return jnp.dot(dispatch.T, expert_out, precision=HIGHEST_PRECISION, preferred_element_type=jnp.float32)

def layer(hidden, attend, output, upward, downward, router, gain_one, gain_two, table, buckets, route_ids, seq_lengths):
    normed = low(rms(hidden, gain_one))
    projected = jnp.einsum('bsd,de->bse', normed, attend, precision=HIGHEST_PRECISION)
    query_rows = low_back(low(projected[..., :D]))
    key_rows = low_back(low(projected[..., D:2 * D]))
    value_rows = low_back(low(projected[..., 2 * D:]))
    attend_one = jax.checkpoint(lambda packed: attention(packed[0], packed[1], packed[2], packed[3], table, buckets))
    mixed = lax.map(attend_one, (query_rows, key_rows, value_rows, seq_lengths))
    mixed = low_back(low(mixed))
    hidden = hidden + low_back(jnp.einsum('bsd,de->bse', mixed, output, precision=HIGHEST_PRECISION))
    normed = low(rms(hidden, gain_two))
    router_logits = low_back(jnp.einsum('bsd,de->bse', normed, router, precision=HIGHEST_PRECISION))
    router_probs = jax.nn.softmax(router_logits, -1)
    onehot = (route_ids[..., None] == jnp.arange(EXPERTS)).astype(jnp.float32)
    gate_value = lax.optimization_barrier(jnp.sum(router_probs * onehot, -1))
    block_rows = normed.reshape(-1, SEQ_DEV, D)
    block_routes = route_ids.reshape(-1, SEQ_DEV)
    expert_one = jax.checkpoint(lambda packed: expert_block(packed[0], packed[1], upward, downward))
    token_out = lax.map(expert_one, (block_rows, block_routes)).reshape(hidden.shape)
    token_out = low_back(token_out)
    return hidden + gate_value[..., None] * token_out

def adam_update(weight, grad, first, second, rate):
    first = BETA_ONE * first + (1.0 - BETA_ONE) * grad
    second = BETA_TWO * second + (1.0 - BETA_TWO) * grad * grad
    mean_hat = first / (1.0 - BETA_ONE ** STEP_COUNT)
    square_hat = second / (1.0 - BETA_TWO ** STEP_COUNT)
    weight = weight - rate * (mean_hat / (jnp.sqrt(square_hat) + ADAM_EPSILON) + WEIGHT_DECAY * weight)
    return (weight, first, second)

def reference(token_ids, lengths, routes, positions, targets, teacher_index, teacher_weight, buckets, embed_weight, embed_mean, embed_square, attend_weight, attend_mean, attend_square, output_weight, output_mean, output_square, upward_weight, upward_mean, upward_square, downward_weight, downward_mean, downward_square, router_weight, router_mean, router_square, gains_weight, gains_mean, gains_square, bias_weight, bias_mean, bias_square):
    params = (embed_weight, attend_weight, output_weight, upward_weight, downward_weight, router_weight, gains_weight, bias_weight)
    means = (embed_mean, attend_mean, output_mean, upward_mean, downward_mean, router_mean, gains_mean, bias_mean)
    squares = (embed_square, attend_square, output_square, upward_square, downward_square, router_square, gains_square, bias_square)
    teacher = teacher_weight / lax.optimization_barrier(jnp.sum(teacher_weight, -1, keepdims=True))
    block_ids = jnp.arange(POSITIONS) // NPOS
    global_pos = block_ids[None, None, :] * SEQ_DEV + positions
    valid = global_pos < lengths[:, :, None]

    def step_loss(*weights):
        embed, attend, output, upward, downward, router, gains, bias = [low(item) for item in weights]
        loss_total = jnp.zeros((), jnp.float32)
        for batch_index in range(MB):
            hidden = embed[token_ids[batch_index]]
            for layer_index in range(LAYERS):
                hidden = layer(hidden, attend[layer_index], output[layer_index], upward[layer_index], downward[layer_index], router[layer_index], gains[2 * layer_index], gains[2 * layer_index + 1], bias[layer_index].reshape(NB, H), buckets, routes[batch_index, :, :, 0], lengths[batch_index])
            final = rms(hidden, gains[2 * LAYERS])
            picked = low(jnp.take_along_axis(final, global_pos[batch_index][..., None], 1))

            def head_rows(packed):
                rows, index_rows, teach_rows, target_rows, valid_rows = packed
                logits = low_back(jnp.dot(rows, embed.T, precision=HIGHEST_PRECISION, preferred_element_type=jnp.float32) * D ** (-0.5))
                log_probs = jax.nn.log_softmax(logits, -1)
                taken = jnp.take_along_axis(log_probs, index_rows, 1)
                target_lp = jnp.take_along_axis(log_probs, target_rows[:, None], 1)[:, 0]
                per_row = lax.optimization_barrier(jnp.sum(teach_rows * (jnp.log(teach_rows) - taken), -1)) - target_lp
                return jnp.sum(jnp.where(valid_rows, per_row, 0.0))
            losses = lax.map(jax.checkpoint(head_rows), (picked, teacher_index[batch_index], teacher[batch_index], targets[batch_index], valid[batch_index]))
            loss_total = loss_total + jnp.sum(losses)
        return loss_total
    loss_value, pullback = jax.vjp(step_loss, *params)
    grads = pullback(jnp.ones_like(loss_value))
    grad_norm = jnp.sqrt(sum((jnp.sum(item * item) for item in grads)))
    factor = jnp.minimum(1.0, CLIP_NORM / (grad_norm + 1e-06))
    results = [loss_value, jnp.sum(valid.astype(jnp.float32)), grad_norm]
    for weight, grad, first, second, rate in zip(params, grads, means, squares, STEP_RATES):
        results.extend(adam_update(weight, grad * factor, first, second, rate))
    return tuple(results)
```

```python
import functools

import jax
import jax.numpy as jnp
from jax import lax
from jax.experimental import pallas as pl
from jax.experimental.pallas import tpu as pltpu
from jax.sharding import PartitionSpec as P

H = 12
HD = 64
STEP_COUNT = 10

EPSILON = 1e-06
ADAM_EPSILON = 1e-08
BETA_ONE = 0.9
BETA_TWO = 0.999
WEIGHT_DECAY = 0.01
CLIP_NORM = 1.0
STEP_RATES = (0.5, 0.03, 0.3, 0.03, 0.04, 0.02, 0.9, 0.5)
HIGHEST_PRECISION = lax.Precision.HIGHEST
VMEM_LIMIT = 48 * 1024 * 1024
BF16 = jnp.bfloat16
F32 = jnp.float32


def matmul(left_side, right_side):
    return jnp.dot(left_side, right_side, preferred_element_type=F32)


def contract(left_side, right_side, left_dim, right_dim):
    return lax.dot_general(
        left_side,
        right_side,
        (((left_dim,), (right_dim,)), ((), ())),
        preferred_element_type=F32,
    )


def rms_norm(hidden, gain):
    norm_scale = lax.rsqrt(jnp.mean(hidden * hidden, -1, keepdims=True) + EPSILON)
    return (hidden * norm_scale * gain, norm_scale)


def rms_back(hidden, norm_scale, gain, upstream):
    normed = hidden * norm_scale
    grad_normed = upstream * gain
    grad_gain = jnp.sum(upstream * normed, 0)
    grad_hidden = norm_scale * (
        grad_normed - normed * jnp.mean(grad_normed * normed, -1, keepdims=True)
    )
    return (grad_hidden, grad_gain)


def bias_tile_kernel(rel_ref, tile_ref):
    heads, width, block = tile_ref.shape
    length = rel_ref.shape[2]
    for head in range(heads):
        spread = jnp.broadcast_to(rel_ref[head], (block, length))
        skewed = pltpu.roll(spread, length - (block - 1), 1, stride=1, stride_axis=0)
        tile_ref[head] = skewed[:, :width].T


def bias_tile(relative, block, total):
    heads, length = relative.shape
    width = 2 * total - block
    padded = jnp.pad(relative, ((0, 0), (0, 2 * total - length)))[:, None, :]
    return pl.pallas_call(
        bias_tile_kernel,
        out_shape=jax.ShapeDtypeStruct((heads, width, block), F32),
        compiler_params=pltpu.CompilerParams(vmem_limit_bytes=VMEM_LIMIT),
        name="bias_tile",
    )(padded)


def head_columns(ref, part, heads, head):
    at = (part * heads + head) * HD
    return jnp.concatenate([ref[index, 0, at : at + HD, :] for index in range(ref.shape[0])], 1)


def transposed_scores(length, key, query_t, tile_ref, head, start, total):
    scores = matmul(key, query_t) * HD ** (-0.5) + tile_ref[head, pl.ds(start, total), :]
    key_ids = lax.broadcasted_iota(jnp.int32, scores.shape, 0)
    return jnp.where(key_ids < length, scores, -1e30)


def attend_kernel(length_ref, qkv_ref, tile_ref, out_ref, lse_ref):
    blocks, _, width, block = qkv_ref.shape
    total = blocks * block
    heads = width // (3 * HD)
    length = length_ref[pl.program_id(0)]
    for head in range(heads):
        at = head * HD
        key = head_columns(qkv_ref, 1, heads, head).T
        value_t = head_columns(qkv_ref, 2, heads, head)

        def step(index, carried, head=head, at=at, key=key, value_t=value_t):
            query_t = qkv_ref[index, 0, at : at + HD, :]
            start = pl.multiple_of((blocks - 1 - index) * block, block)
            scores = transposed_scores(length, key, query_t, tile_ref, head, start, total)
            peak = jnp.max(scores, 0, keepdims=True)
            powers = jnp.exp(scores - peak)
            norm = jnp.sum(powers, 0, keepdims=True)
            weights = (powers * (1.0 / norm)).astype(BF16)
            out_ref[index, 0, at : at + HD, :] = matmul(value_t, weights).astype(BF16)
            lse_ref[0, pl.ds(head * blocks + index, 1), :] = peak + jnp.log(norm)
            return carried

        lax.fori_loop(0, blocks, step, 0)


def attend(qkv, tile, lengths):
    blocks, count, width, block = qkv.shape
    heads = width // (3 * HD)
    total = blocks * block
    return pl.pallas_call(
        attend_kernel,
        grid=(count,),
        in_specs=[
            pl.BlockSpec(memory_space=pltpu.SMEM),
            pl.BlockSpec((blocks, 1, width, block), lambda i: (0, i, 0, 0)),
            pl.BlockSpec(tile.shape, lambda i: (0, 0, 0)),
        ],
        out_specs=[
            pl.BlockSpec((blocks, 1, heads * HD, block), lambda i: (0, i, 0, 0)),
            pl.BlockSpec((1, heads * blocks, block), lambda i: (i, 0, 0)),
        ],
        out_shape=[
            jax.ShapeDtypeStruct((blocks, count, heads * HD, block), BF16),
            jax.ShapeDtypeStruct((count, heads * blocks, block), F32),
        ],
        compiler_params=pltpu.CompilerParams(vmem_limit_bytes=VMEM_LIMIT),
        cost_estimate=pl.CostEstimate(
            flops=4 * count * heads * total * total * HD,
            bytes_accessed=2 * qkv.size + 4 * tile.size,
            transcendentals=count * heads * total * total,
        ),
        name="attend",
    )(lengths, qkv, tile)


def attend_back_kernel(
    length_ref, qkv_ref, out_grad_ref, lse_ref, tile_ref, grad_ref, rel_ref, sums_ref, dk_ref, dv_ref
):
    blocks, _, width, block = qkv_ref.shape
    total = blocks * block
    heads = width // (3 * HD)
    count = pl.num_programs(0)
    length = length_ref[pl.program_id(0)]
    scale = HD ** (-0.5)

    @pl.when(pl.program_id(0) == 0)
    def _():
        sums_ref[...] = jnp.zeros_like(sums_ref)

    for head in range(heads):
        at = head * HD
        key_t = head_columns(qkv_ref, 1, heads, head)
        key = key_t.T
        value = head_columns(qkv_ref, 2, heads, head).T
        dk_ref[...] = jnp.zeros_like(dk_ref)
        dv_ref[...] = jnp.zeros_like(dv_ref)

        def step(index, carried, head=head, at=at, key=key, key_t=key_t, value=value):
            query_t = qkv_ref[index, 0, at : at + HD, :]
            upstream_t = out_grad_ref[index, 0, at : at + HD, :]
            start = pl.multiple_of((blocks - 1 - index) * block, block)
            scores = transposed_scores(length, key, query_t, tile_ref, head, start, total)
            weights = jnp.exp(scores - lse_ref[0, pl.ds(head * blocks + index, 1), :])
            grad_weights = matmul(value, upstream_t)
            product = weights * grad_weights
            delta = jnp.sum(product, 0, keepdims=True)
            grad_scores = (product - weights * delta).astype(BF16)
            grad_ref[index, 0, at : at + HD, :] = (matmul(key_t, grad_scores) * scale).astype(BF16)
            dk_ref[...] += contract(query_t, grad_scores, 1, 1)
            dv_ref[...] += contract(upstream_t, weights.astype(BF16), 1, 1)
            sums_ref[head, pl.ds(start, total), :] += grad_scores.astype(F32)
            return carried

        lax.fori_loop(0, blocks, step, 0)
        key_at, value_at = heads * HD + at, 2 * heads * HD + at
        for index in range(blocks):
            columns = slice(index * block, (index + 1) * block)
            grad_ref[index, 0, key_at : key_at + HD, :] = (dk_ref[:, columns] * scale).astype(BF16)
            grad_ref[index, 0, value_at : value_at + HD, :] = dv_ref[:, columns].astype(BF16)

    @pl.when(pl.program_id(0) == count - 1)
    def _():
        length_all = 2 * total
        for head in range(heads):
            rows = jnp.concatenate([jnp.zeros((block, block), F32), sums_ref[head].T], 1)
            half = block // 2
            while half >= 8:
                rows = rows[:half] + pltpu.roll(rows[half:], length_all - half, 1)
                half //= 2
            folded = rows[:1]
            for row in range(1, 8):
                folded = folded + pltpu.roll(rows, length_all - row, 1)[row : row + 1]
            rel_ref[head] = folded


def attend_back(qkv, out_grad, lse, tile, lengths):
    blocks, count, width, block = qkv.shape
    heads = width // (3 * HD)
    total = blocks * block
    grads, rel = pl.pallas_call(
        attend_back_kernel,
        grid=(count,),
        in_specs=[
            pl.BlockSpec(memory_space=pltpu.SMEM),
            pl.BlockSpec((blocks, 1, width, block), lambda i: (0, i, 0, 0)),
            pl.BlockSpec((blocks, 1, heads * HD, block), lambda i: (0, i, 0, 0)),
            pl.BlockSpec((1, heads * blocks, block), lambda i: (i, 0, 0)),
            pl.BlockSpec(tile.shape, lambda i: (0, 0, 0)),
        ],
        out_specs=[
            pl.BlockSpec((blocks, 1, width, block), lambda i: (0, i, 0, 0)),
            pl.BlockSpec((heads, 1, 2 * total), lambda i: (0, 0, 0)),
        ],
        out_shape=[
            jax.ShapeDtypeStruct((blocks, count, width, block), BF16),
            jax.ShapeDtypeStruct((heads, 1, 2 * total), F32),
        ],
        scratch_shapes=[
            pltpu.VMEM(tile.shape, F32),
            pltpu.VMEM((HD, total), F32),
            pltpu.VMEM((HD, total), F32),
        ],
        compiler_params=pltpu.CompilerParams(vmem_limit_bytes=VMEM_LIMIT),
        cost_estimate=pl.CostEstimate(
            flops=10 * count * heads * total * total * HD,
            bytes_accessed=4 * qkv.size + 4 * tile.size,
            transcendentals=count * heads * total * total,
        ),
        name="attend_back",
    )(lengths, qkv, out_grad, lse, tile)
    return (grads, rel[:, 0, 1:])


def project_kernel(hidden_ref, gain_ref, weight_ref, out_ref, normed_ref, scale_ref):
    ways, _, width, _ = out_ref.shape
    normed, scale = rms_norm(hidden_ref[0], gain_ref[...])
    normed = normed.astype(BF16)
    normed_ref[0] = normed
    scale_ref[0] = scale
    for way in range(ways):
        columns = weight_ref[:, way * width : (way + 1) * width]
        out_ref[way, 0] = matmul(normed, columns).astype(BF16).T


def project(hidden, gain, dense, ways):
    count, rows, width = hidden.shape
    part = 3 * width // ways
    return pl.pallas_call(
        project_kernel,
        grid=(count,),
        in_specs=[
            pl.BlockSpec((1, rows, width), lambda i: (i, 0, 0)),
            pl.BlockSpec((1, width), lambda i: (0, 0)),
            pl.BlockSpec((width, 3 * width), lambda i: (0, 0)),
        ],
        out_specs=[
            pl.BlockSpec((ways, 1, part, rows), lambda i: (0, i, 0, 0)),
            pl.BlockSpec((1, rows, width), lambda i: (i, 0, 0)),
            pl.BlockSpec((1, rows, 1), lambda i: (i, 0, 0)),
        ],
        out_shape=[
            jax.ShapeDtypeStruct((ways, count, part, rows), BF16),
            jax.ShapeDtypeStruct((count, rows, width), BF16),
            jax.ShapeDtypeStruct((count, rows, 1), F32),
        ],
        compiler_params=pltpu.CompilerParams(vmem_limit_bytes=VMEM_LIMIT),
        cost_estimate=pl.CostEstimate(
            flops=6 * count * rows * width * width,
            bytes_accessed=12 * count * rows * width + 6 * width * width,
            transcendentals=0,
        ),
        name="project",
    )(hidden, gain[None], dense)


def embed_adam_kernel(rate, clip_ref, grad_ref, weight_ref, first_ref, second_ref, *out_refs):
    grad = jnp.concatenate([grad_ref[way].T for way in range(grad_ref.shape[0])], 1).astype(F32)
    updated = adam_update(
        weight_ref[...], grad * clip_ref[0], first_ref[...], second_ref[...], rate
    )
    for ref, value in zip(out_refs, updated):
        ref[...] = value


def embed_adam(weight, grad, first, second, clip, rate):
    rows, width = weight.shape
    ways, part, _ = grad.shape
    block = min(256, rows)
    state = pl.BlockSpec((block, width), lambda i: (i, 0))
    return pl.pallas_call(
        functools.partial(embed_adam_kernel, rate),
        grid=(pl.cdiv(rows, block),),
        in_specs=[
            pl.BlockSpec(memory_space=pltpu.SMEM),
            pl.BlockSpec((ways, part, block), lambda i: (0, 0, i)),
            state,
            state,
            state,
        ],
        out_specs=[state, state, state],
        out_shape=[jax.ShapeDtypeStruct((rows, width), F32)] * 3,
        compiler_params=pltpu.CompilerParams(vmem_limit_bytes=VMEM_LIMIT),
        cost_estimate=pl.CostEstimate(
            flops=20 * rows * width, bytes_accessed=26 * rows * width, transcendentals=rows * width
        ),
        name="embed_adam",
    )(clip.reshape(1), grad, weight, first, second)


def exchange(parts):
    return lax.all_to_all(parts, "seq", split_axis=0, concat_axis=0, tiled=True)


def share(part):
    ways = lax.axis_size("seq")
    return exchange(jnp.broadcast_to(part[None], (ways,) + part.shape))


def sum_over_seq(parts):
    return jnp.sum(exchange(parts).astype(F32), 0)


def as_rows(flat):
    return jnp.pad(flat, (0, -flat.size % 1024)).reshape(-1, 128)


def sum_everywhere(parts):
    ways, owners = parts.shape[:2]
    size = parts.size // (ways * owners)
    flat = parts.reshape(ways * owners, size)
    flat = jnp.pad(flat, ((0, 0), (0, -size % 1024))).reshape(ways * owners, -1, 128)
    moved = lax.all_to_all(flat, ("seq", "fsdp"), split_axis=0, concat_axis=0, tiled=True)
    return jnp.sum(moved, 0).reshape(-1)[:size]


def after(value, *others):
    return lax.optimization_barrier((value,) + others)


def layer_forward(hidden, weights, gain_one, gain_two, router_w, tile, moe, lengths):
    dense, upward_w, downward_w = weights
    count, rows, width = hidden.shape
    output_w = dense[:, 3 * width :]
    ways = lax.axis_size("seq")
    dispatch, onehot = moe
    slots = dispatch.shape[1]
    projected, normed_one, scale_one = project(hidden, gain_one, dense, ways)
    qkv = exchange(projected)
    mixed, lse = attend(qkv, tile, lengths)
    mixed_t = exchange(mixed).reshape(width, rows)
    after_attn = hidden + contract(mixed_t, output_w, 0, 0).reshape(hidden.shape)
    normed_two, scale_two = rms_norm(after_attn, gain_two)
    normed_two = normed_two.astype(BF16)
    router_probs = jax.nn.softmax(
        matmul(normed_two.reshape(count * rows, width), router_w).reshape(count, rows, -1), -1
    )
    gate = jnp.sum(router_probs * onehot, -1, keepdims=True)
    sent = jnp.einsum("nst,ntd->nsd", dispatch, normed_two, preferred_element_type=F32).astype(BF16)
    sent = sent.reshape(count, ways, slots // ways, width).transpose(1, 0, 2, 3)
    expert_rows = exchange(sent).reshape(count * slots, width)
    upward = matmul(expert_rows, upward_w)
    activated = jax.nn.gelu(upward).astype(BF16)
    expert_out = matmul(activated, downward_w).astype(BF16)
    back = exchange(expert_out.reshape(ways, count, slots // ways, width))
    back = back.transpose(1, 0, 2, 3).reshape(count, slots, width)
    token_out = jnp.einsum("nst,nsd->ntd", dispatch, back, preferred_element_type=F32)
    result = after_attn + gate * token_out
    kept = dict(
        hidden=hidden,
        scale_one=scale_one,
        normed_one=normed_one,
        qkv=qkv,
        lse=lse,
        mixed_t=mixed_t,
        after_attn=after_attn,
        scale_two=scale_two,
        normed_two=normed_two,
        router_probs=router_probs,
        gate=gate,
        expert_rows=expert_rows,
        upward=upward,
        activated=activated,
        token_out=token_out,
    )
    return (result, kept)


def layer_backward(
    grad_out, kept, weights, gain_one, gain_two, router_w, tile, moe, lengths, gates
):
    dense, upward_w, downward_w = weights
    count, rows, width = grad_out.shape
    attend_w, output_w = dense[:, : 3 * width], dense[:, 3 * width :]
    ways = lax.axis_size("seq")
    dispatch, onehot = moe
    slots = dispatch.shape[1]
    flat = (count * rows, width)
    grad_gate = jnp.sum(grad_out * kept["token_out"], -1, keepdims=True)
    grad_token = (kept["gate"] * grad_out).astype(BF16)
    sent = jnp.einsum("nst,ntd->nsd", dispatch, grad_token, preferred_element_type=F32).astype(BF16)
    sent = sent.reshape(count, ways, slots // ways, width).transpose(1, 0, 2, 3)
    grad_expert = exchange(sent).reshape(count * slots, width)
    grad_activated = contract(grad_expert, downward_w, 1, 1)
    grad_upward = jax.vjp(jax.nn.gelu, kept["upward"])[1](grad_activated)[0].astype(BF16)
    grad_rows = contract(grad_upward, upward_w, 1, 1).astype(BF16)
    back = exchange(grad_rows.reshape(ways, count, slots // ways, width))
    back, *first_gate = after(back, *gates[0])
    back = back.transpose(1, 0, 2, 3).reshape(count, slots, width)
    grad_normed = jnp.einsum("nst,nsd->ntd", dispatch, back, preferred_element_type=F32)
    grad_probs = onehot * grad_gate
    router_probs = kept["router_probs"]
    grad_logits = (
        router_probs * (grad_probs - jnp.sum(grad_probs * router_probs, -1, keepdims=True))
    ).astype(BF16)
    grad_logits = grad_logits.reshape(count * rows, -1)
    grad_router = contract(kept["normed_two"].reshape(flat), grad_logits, 0, 0)
    grad_normed = grad_normed.reshape(flat) + contract(grad_logits, router_w, 1, 1)
    grad_mid, grad_gain_two = rms_back(
        kept["after_attn"].reshape(flat), kept["scale_two"].reshape(-1, 1), gain_two, grad_normed
    )
    grad_mid = grad_mid + grad_out.reshape(flat)
    grad_attn = grad_mid.astype(BF16)
    grad_mixed_t = contract(output_w, grad_attn, 1, 1).astype(BF16)
    grad_mixed_t = exchange(grad_mixed_t.reshape(ways, 1, width // ways, rows))
    grad_mixed_t, *second_gate = after(grad_mixed_t, *gates[1])
    grad_qkv, grad_relative = attend_back(kept["qkv"], grad_mixed_t, kept["lse"], tile, lengths)
    grad_projected_t = exchange(grad_qkv).reshape(3 * width, rows)
    grad_first, grad_gain_one = rms_back(
        kept["hidden"].reshape(flat),
        kept["scale_one"].reshape(-1, 1),
        gain_one,
        contract(grad_projected_t, attend_w, 0, 1),
    )
    return (
        (grad_mid + grad_first).reshape(grad_out.shape),
        (
            (kept["expert_rows"], grad_upward),
            (kept["activated"], grad_expert),
            (kept["normed_one"].reshape(flat), grad_projected_t),
            (kept["mixed_t"], grad_attn),
        ),
        (grad_gain_one, grad_gain_two, grad_router, grad_relative),
        (first_gate, second_gate),
    )


def adam_update(weight, grad, first, second, rate):
    first = BETA_ONE * first + (1.0 - BETA_ONE) * grad
    second = BETA_TWO * second + (1.0 - BETA_TWO) * grad * grad
    mean_hat = first / (1.0 - BETA_ONE**STEP_COUNT)
    square_hat = second / (1.0 - BETA_TWO**STEP_COUNT)
    weight = weight - rate * (
        mean_hat / (jnp.sqrt(square_hat) + ADAM_EPSILON) + WEIGHT_DECAY * weight
    )
    return (weight, first, second)


def scatter_owners(item):
    return lax.psum_scatter(item, "fsdp", scatter_dimension=0, tiled=True)


def sum_squares(*arrays):
    return sum(jnp.sum(jnp.square(item.astype(F32))) for item in arrays)


def per_device(
    token_ids,
    lengths,
    routes,
    positions,
    targets,
    teacher_index,
    teacher_weight,
    buckets,
    embed_weight,
    embed_mean,
    embed_square,
    attend_weight,
    attend_mean,
    attend_square,
    output_weight,
    output_mean,
    output_square,
    upward_weight,
    upward_mean,
    upward_square,
    downward_weight,
    downward_mean,
    downward_square,
    router_weight,
    router_mean,
    router_square,
    gains_weight,
    gains_mean,
    gains_square,
    bias_weight,
    bias_mean,
    bias_square,
):
    ways, owners = lax.axis_size("seq"), lax.axis_size("fsdp")
    seq_index, owner_index = lax.axis_index("seq"), lax.axis_index("fsdp")
    layers, experts = upward_weight.shape[0], upward_weight.shape[1]
    vocab_rows, width = embed_weight.shape
    count, rows = token_ids.shape[0], token_ids.shape[2]
    total = rows * ways
    picks = positions.shape[2]
    shard = upward_weight.shape[2]
    part = width // ways
    capacity = rows * 3 // 8
    factor = width ** (-0.5)
    lengths = lengths[:, 0]

    def dense_shard(layer):
        attend_low = attend_weight[layer].reshape(shard, 3, ways, part).transpose(0, 2, 1, 3)
        return jnp.concatenate(
            [attend_low.reshape(shard, 3 * width).astype(BF16), output_weight[layer].astype(BF16)], 1
        )

    def gather_owners(item):
        return lax.all_gather(item, "fsdp", axis=0, tiled=True)

    def gather_expert(item, layer):
        mine = lax.dynamic_index_in_dim(item[layer], seq_index, 0, False)
        return gather_owners(mine.astype(BF16))

    first_dense = dense_shard(0)
    own_ids, first_dense = after(token_ids[:, 0], first_dense)
    first_dense = gather_owners(first_dense)
    group_ids = lax.all_gather(own_ids, "fsdp", axis=0, tiled=False)
    embed_low = embed_weight.astype(BF16)
    vocab_ids = jnp.arange(vocab_rows)
    founds = []
    for batch in range(count):
        local_ids = group_ids[:, batch].reshape(-1) - owner_index * vocab_rows
        founds.append(
            matmul((local_ids[:, None] == vocab_ids[None, :]).astype(BF16), embed_low).astype(BF16)
        )
        if batch == 0:
            founds[0], first_dense = after(founds[0], first_dense)
    later = (attend_weight, output_weight, upward_weight, downward_weight)
    founds[-1], *later = after(founds[-1], *later)
    hiddens = [
        lax.psum_scatter(
            found.reshape(owners, rows, width), "fsdp", scatter_dimension=0, tiled=False
        )
        .astype(F32)
        .reshape(1, rows, width)
        for found in founds
    ]
    weights = []
    for layer in range(layers):
        weights.append(
            (
                gather_owners(dense_shard(layer)) if layer else first_dense,
                gather_expert(later[2], layer),
                gather_expert(later[3], layer),
            )
        )

    valid_own = (seq_index * rows + positions[:, 0] < lengths[:, None]).astype(F32)
    teacher_own = teacher_weight[:, 0] / jnp.sum(teacher_weight[:, 0], -1, keepdims=True)
    small = jnp.concatenate(
        [
            lax.optimization_barrier(item.astype(BF16)).astype(F32).reshape(-1)
            for item in (gains_weight, bias_weight, router_weight)
        ]
        + [item.astype(F32).reshape(-1) for item in (valid_own, targets, teacher_index, teacher_own)]
    )
    small = lax.all_gather(as_rows(small), "fsdp", axis=0, tiled=False).reshape(owners, -1)
    pieces, at = [], 0
    for item in (gains_weight, bias_weight, router_weight, valid_own, targets, teacher_index, teacher_own):
        pieces.append(small[:, at : at + item.size])
        at += item.size
    norms = 2 * layers + 1
    gains_full = pieces[0].reshape(owners, norms, shard).transpose(1, 0, 2).reshape(norms, width)
    bias_full = pieces[1].reshape(owners, layers, -1).transpose(1, 0, 2).reshape(layers, -1, H)
    router_full = (
        pieces[2].reshape(owners, layers, shard, experts).transpose(1, 0, 2, 3).astype(BF16)
    ).reshape(layers, width, experts)
    valid_all = pieces[3].reshape(-1)
    targets_all = pieces[4].astype(jnp.int32).reshape(-1, 1)
    index_all = pieces[5].astype(jnp.int32).reshape(-1, teacher_index.shape[3])
    teacher_all = pieces[6].reshape(-1, teacher_index.shape[3])

    head_local = H // ways
    local_tables = lax.dynamic_slice_in_dim(bias_full, seq_index * head_local, head_local, 2)
    onehot_buckets = (buckets[:, None] == jnp.arange(bias_full.shape[1])[None, :]).astype(F32)
    tiles = [
        bias_tile(
            jnp.dot(onehot_buckets, local_tables[layer], precision=HIGHEST_PRECISION).T, rows, total
        )
        for layer in range(layers)
    ]

    route_ids = routes[:, 0, :, 0]
    onehot = (route_ids[..., None] == jnp.arange(experts)).astype(F32)
    ranks = jnp.sum((jnp.cumsum(onehot, 1) - 1.0) * onehot, -1).astype(jnp.int32)
    slot_index = route_ids * capacity + ranks
    dispatch = (slot_index[:, None, :] == jnp.arange(experts * capacity)[None, :, None]).astype(BF16)

    base = owner_index * vocab_rows
    entry = jnp.concatenate([index_all, targets_all], 1) - base
    mass = jnp.concatenate([teacher_all, jnp.ones_like(teacher_all[:, :1])], 1)
    lanes = 128
    groups = -(-vocab_rows // lanes)
    entry = jnp.where((entry >= 0) & (entry < vocab_rows), entry, groups * lanes)
    high = (entry[..., None] // lanes == jnp.arange(groups)).astype(F32) * mass[..., None]
    low = (entry[..., None] % lanes == jnp.arange(lanes)).astype(F32)
    wanted = jnp.einsum("rkh,rkl->rhl", high, low, precision=HIGHEST_PRECISION)
    wanted = wanted.reshape(-1, groups * lanes)[:, :vocab_rows]
    mass_all = jnp.sum(teacher_all, -1, keepdims=True) + 1.0

    kept_all = [[None] * count for layer in range(layers)]
    moes = [(dispatch[batch : batch + 1], onehot[batch : batch + 1]) for batch in range(count)]
    used = [lengths[batch : batch + 1] for batch in range(count)]
    for layer in range(layers):
        for batch in range(count):
            hiddens[batch], kept_all[layer][batch] = layer_forward(
                hiddens[batch],
                weights[layer],
                gains_full[2 * layer],
                gains_full[2 * layer + 1],
                router_full[layer],
                tiles[layer],
                moes[batch],
                used[batch],
            )
        if layer == 0:
            hiddens[-1], wanted = after(hiddens[-1], wanted)
    hidden = jnp.concatenate(hiddens, 0)

    final, scale_final = rms_norm(hidden, gains_full[2 * layers])
    chosen = (positions[:, 0][..., None] == jnp.arange(rows)).astype(BF16)
    picked = jnp.einsum("npt,ntd->npd", chosen, final.astype(BF16), preferred_element_type=F32)
    picked = lax.all_gather(
        picked.astype(BF16).reshape(count * picks, width), "fsdp", axis=0, tiled=True
    )
    logits = contract(picked, embed_low, 1, 1) * factor
    peak = jnp.max(logits, -1)
    stats = jnp.stack([peak, jnp.sum(jnp.exp(logits - peak[:, None]), -1)])
    stats = lax.all_gather(stats, "fsdp", axis=0, tiled=False)
    peak_all = jnp.max(stats[:, 0], 0)
    lse_all = peak_all + jnp.log(jnp.sum(stats[:, 1] * jnp.exp(stats[:, 0] - peak_all), 0))
    grad_logits = mass_all * jnp.exp(logits - lse_all[:, None]) - wanted
    grad_logits = (grad_logits * valid_all[:, None]).astype(BF16)
    lse_own = lax.dynamic_slice_in_dim(lse_all, owner_index * count * picks, count * picks, 0)
    mass_own = jnp.sum(teacher_own, -1) + 1.0
    own_rows = jnp.sum(teacher_own * jnp.log(teacher_own), -1) + mass_own * lse_own.reshape(count, picks)
    loss_part = jnp.sum(valid_own * own_rows) - jnp.sum(
        valid_all * jnp.sum(wanted * logits, -1)
    )
    grad_picked = lax.psum_scatter(
        matmul(grad_logits, embed_low), "fsdp", scatter_dimension=0, tiled=True
    )
    grad_picked = (grad_picked * factor).reshape(count, picks, width)
    head_grad = (contract(picked, grad_logits, 0, 0) * factor).astype(BF16)
    head_grad = sum_over_seq(head_grad.reshape(ways, part, vocab_rows))
    grad_final = jnp.einsum(
        "npt,npd->ntd", chosen.astype(F32), grad_picked, precision=HIGHEST_PRECISION
    )
    grad_hidden, grad_gain_final = rms_back(
        hidden.reshape(count * rows, width),
        scale_final.reshape(-1, 1),
        gains_full[2 * layers],
        grad_final.reshape(count * rows, width),
    )
    grad_hidden = grad_hidden.reshape(hidden.shape)
    grad_hiddens = [grad_hidden[batch : batch + 1] for batch in range(count)]

    gain_grads = [None] * norms
    gain_grads[2 * layers] = grad_gain_final
    router_grads, table_grads = [None] * layers, [None] * layers
    grad_parts = [None] * layers
    gates = []
    for layer in reversed(range(layers)):
        sides, small_grads = [None] * count, [None] * count
        passed = []
        for batch in range(count):
            held = gates[2 * batch : 2 * batch + 2]
            held = [held[at : at + 1] for at in range(2)]
            grad_hiddens[batch], sides[batch], small_grads[batch], held = layer_backward(
                grad_hiddens[batch],
                kept_all[layer][batch],
                weights[layer],
                gains_full[2 * layer],
                gains_full[2 * layer + 1],
                router_full[layer],
                tiles[layer],
                moes[batch],
                used[batch],
                held,
            )
            passed.extend(held[0] + held[1])
        if passed:
            grad_parts[layer + 1] = passed
        gain_grads[2 * layer], gain_grads[2 * layer + 1], router_grads[layer], grad_relative = (
            sum(items) for items in zip(*small_grads)
        )
        table_grads[layer] = jnp.dot(onehot_buckets.T, grad_relative.T, precision=HIGHEST_PRECISION)
        weight_grads = [
            contract(
                jnp.concatenate([item[0] for item in pairs], left_dim),
                jnp.concatenate([item[1] for item in pairs], right_dim),
                left_dim,
                right_dim,
            ).astype(BF16)
            for pairs, left_dim, right_dim in zip(zip(*sides), (0, 0, 0, 1), (0, 0, 1, 0))
        ]
        grad_parts[layer] = [scatter_owners(item) for item in weight_grads[:2]]
        dense_grad = jnp.concatenate(weight_grads[2:], 1)
        if layer:
            grad_parts[layer].append(scatter_owners(dense_grad))
        gates = grad_parts[layer]
        if layer:
            grad_hiddens[0], dense_grad = after(grad_hiddens[0], dense_grad)

    moved = []
    for batch in range(count):
        if batch < 2:
            grad_hiddens[batch], grad_parts[0][batch] = after(
                grad_hiddens[batch], grad_parts[0][batch]
            )
        columns = grad_hiddens[batch].reshape(rows, width).astype(BF16).T
        columns = exchange(columns.reshape(ways, part, rows))
        columns = lax.all_gather(columns, "fsdp", axis=0, tiled=False)
        moved.append(columns.transpose(2, 0, 1, 3).reshape(part, -1))
    moved[0], dense_grad = after(moved[0], dense_grad)
    grad_parts[0].append(scatter_owners(dense_grad))
    shared = [[None] * 3 for layer in range(layers)]
    shared[-1] = [share(item) for item in grad_parts[-1][:2]]
    moved[-1], *shared[-1] = after(moved[-1], *shared[-1])
    every_id = lax.all_gather(group_ids, "seq", axis=0, tiled=False) - owner_index * vocab_rows
    every_id = every_id.transpose(2, 1, 0, 3).reshape(count, -1)
    embed_part = head_grad
    for batch in range(count):
        embed_part = embed_part + matmul(
            moved[batch], (every_id[batch][:, None] == vocab_ids[None, :]).astype(BF16)
        )
    embed_part = embed_part.astype(BF16)
    for layer in range(layers):
        dense = grad_parts[layer][2]
        dense = jnp.concatenate(
            [
                dense[:, : 3 * width].reshape(shard, ways, 3 * part),
                dense[:, 3 * width :].reshape(shard, ways, part),
            ],
            2,
        )
        grad_parts[layer][2] = sum_over_seq(dense.transpose(1, 0, 2)).astype(BF16)

    tables = lax.dynamic_update_slice(
        jnp.zeros(bias_full.shape, F32), jnp.stack(table_grads), (0, 0, seq_index * head_local)
    )
    bias_shard = bias_weight.shape[1]
    tiny = jnp.concatenate(
        [
            jnp.stack(gain_grads).reshape(norms, owners, shard).transpose(1, 0, 2).reshape(owners, -1),
            tables.reshape(layers, owners, bias_shard).transpose(1, 0, 2).reshape(owners, -1),
            jnp.stack(router_grads)
            .reshape(layers, owners, shard, experts)
            .transpose(1, 0, 2, 3)
            .reshape(owners, -1),
            jnp.broadcast_to(jnp.stack([loss_part, jnp.sum(valid_own)])[None], (owners, 2)),
        ],
        1,
    )
    tiny = sum_everywhere(jnp.broadcast_to(tiny[None], (ways,) + tiny.shape))
    gain_size, bias_size = gains_weight.size, bias_weight.size
    gains_grad = tiny[:gain_size].reshape(gains_weight.shape)
    bias_grad = tiny[gain_size : gain_size + bias_size].reshape(bias_weight.shape)
    router_grad = tiny[gain_size + bias_size : -2].reshape(router_weight.shape)
    loss_value, loss_count = tiny[-2], tiny[-1]

    squares_part = (
        sum_squares(embed_part, *(item for parts in grad_parts for item in parts))
        + sum_squares(gains_grad, bias_grad, router_grad) / ways
    )
    grad_norm = jnp.sqrt(
        sum_everywhere(jnp.broadcast_to(squares_part, (ways, owners, 1)))[0]
    )
    clip_factor = jnp.minimum(1.0, CLIP_NORM / (grad_norm + 1e-06))

    embed_grad = share(embed_part)
    for layer in range(layers):
        shared[layer] = [
            share(item) if done is None else done for item, done in zip(grad_parts[layer], (shared[layer] + [None])[:3])
        ]
    upward_grad = jnp.stack([items[0] for items in shared])
    downward_grad = jnp.stack([items[1] for items in shared])
    dense_grads = [items[2] for items in shared]
    attend_grad = jnp.stack(
        [
            item[:, :, : 3 * part]
            .reshape(ways, shard, 3, part)
            .transpose(1, 2, 0, 3)
            .reshape(shard, 3 * width)
            for item in dense_grads
        ]
    )
    output_grad = jnp.stack(
        [item[:, :, 3 * part :].transpose(1, 0, 2).reshape(shard, width) for item in dense_grads]
    )
    grads = (
        embed_grad,
        attend_grad,
        output_grad,
        upward_grad,
        downward_grad,
        router_grad,
        gains_grad,
        bias_grad,
    )
    params = (
        embed_weight,
        attend_weight,
        output_weight,
        upward_weight,
        downward_weight,
        router_weight,
        gains_weight,
        bias_weight,
    )
    means = (
        embed_mean,
        attend_mean,
        output_mean,
        upward_mean,
        downward_mean,
        router_mean,
        gains_mean,
        bias_mean,
    )
    squares = (
        embed_square,
        attend_square,
        output_square,
        upward_square,
        downward_square,
        router_square,
        gains_square,
        bias_square,
    )
    results = [loss_value, loss_count, grad_norm]
    results.extend(
        embed_adam(embed_weight, embed_grad, embed_mean, embed_square, clip_factor, STEP_RATES[0])
    )
    for weight, grad, first, second, rate in list(
        zip(params, grads, means, squares, STEP_RATES)
    )[1:]:
        results.extend(adam_update(weight, grad.astype(F32) * clip_factor, first, second, rate))
    return tuple(results)


def solution(mesh):
    token = P(None, "fsdp", "seq")
    entry = P(None, "fsdp", "seq", None)
    state = (
        [P("fsdp", None)] * 3
        + [P(None, "fsdp", None)] * 6
        + [P(None, None, "fsdp", None)] * 6
        + [P(None, "fsdp", None)] * 3
        + [P(None, "fsdp")] * 6
    )
    return jax.shard_map(
        per_device,
        mesh=mesh,
        in_specs=tuple([token, P(None, "fsdp"), entry, token, token, entry, entry, P()] + state),
        out_specs=tuple([P(), P(), P()] + state),
        check_vma=False,
    )
```

```python
import functools

import jax
import jax.numpy as jnp
from jax import lax
from jax.experimental import pallas as pl
from jax.experimental.pallas import tpu as pltpu
from jax.sharding import PartitionSpec as P

H = 12
HD = 64
STEP_COUNT = 10

EPSILON = 1e-06
ADAM_EPSILON = 1e-08
BETA_ONE = 0.9
BETA_TWO = 0.999
WEIGHT_DECAY = 0.01
CLIP_NORM = 1.0
STEP_RATES = (0.5, 0.03, 0.3, 0.03, 0.04, 0.02, 0.9, 0.5)
HIGHEST_PRECISION = lax.Precision.HIGHEST
VMEM_LIMIT = 48 * 1024 * 1024
BF16 = jnp.bfloat16
F32 = jnp.float32


def matmul(left_side, right_side):
    return jnp.dot(left_side, right_side, preferred_element_type=F32)


def contract(left_side, right_side, left_dim, right_dim):
    return lax.dot_general(
        left_side,
        right_side,
        (((left_dim,), (right_dim,)), ((), ())),
        preferred_element_type=F32,
    )


def rms_norm(hidden, gain):
    norm_scale = lax.rsqrt(jnp.mean(hidden * hidden, -1, keepdims=True) + EPSILON)
    return (hidden * norm_scale * gain, norm_scale)


def rms_back(hidden, norm_scale, gain, upstream):
    normed = hidden * norm_scale
    grad_normed = upstream * gain
    grad_gain = jnp.sum(upstream * normed, 0)
    grad_hidden = norm_scale * (
        grad_normed - normed * jnp.mean(grad_normed * normed, -1, keepdims=True)
    )
    return (grad_hidden, grad_gain)


def bias_tile_kernel(rel_ref, tile_ref):
    heads, width, block = tile_ref.shape
    length = rel_ref.shape[2]
    for head in range(heads):
        spread = jnp.broadcast_to(rel_ref[head], (block, length))
        skewed = pltpu.roll(spread, length - (block - 1), 1, stride=1, stride_axis=0)
        tile_ref[head] = skewed[:, :width].T


def bias_tile(relative, block, total):
    heads, length = relative.shape
    width = 2 * total - block
    padded = jnp.pad(relative, ((0, 0), (0, 2 * total - length)))[:, None, :]
    return pl.pallas_call(
        bias_tile_kernel,
        out_shape=jax.ShapeDtypeStruct((heads, width, block), F32),
        compiler_params=pltpu.CompilerParams(vmem_limit_bytes=VMEM_LIMIT),
        name="bias_tile",
    )(padded)


def head_columns(ref, part, heads, head):
    at = (part * heads + head) * HD
    return jnp.concatenate([ref[index, 0, at : at + HD, :] for index in range(ref.shape[0])], 1)


def transposed_scores(length, key, query_t, tile_ref, head, start, total):
    scores = matmul(key, query_t) * HD ** (-0.5) + tile_ref[head, pl.ds(start, total), :]
    key_ids = lax.broadcasted_iota(jnp.int32, scores.shape, 0)
    return jnp.where(key_ids < length, scores, -1e30)


def attend_kernel(length_ref, qkv_ref, tile_ref, out_ref, lse_ref):
    blocks, _, width, block = qkv_ref.shape
    total = blocks * block
    heads = width // (3 * HD)
    length = length_ref[pl.program_id(0)]
    for head in range(heads):
        at = head * HD
        key = head_columns(qkv_ref, 1, heads, head).T
        value_t = head_columns(qkv_ref, 2, heads, head)

        def step(index, carried, head=head, at=at, key=key, value_t=value_t):
            query_t = qkv_ref[index, 0, at : at + HD, :]
            start = pl.multiple_of((blocks - 1 - index) * block, block)
            scores = transposed_scores(length, key, query_t, tile_ref, head, start, total)
            peak = jnp.max(scores, 0, keepdims=True)
            powers = jnp.exp(scores - peak)
            norm = jnp.sum(powers, 0, keepdims=True)
            weights = (powers * (1.0 / norm)).astype(BF16)
            out_ref[index, 0, at : at + HD, :] = matmul(value_t, weights).astype(BF16)
            lse_ref[0, pl.ds(head * blocks + index, 1), :] = peak + jnp.log(norm)
            return carried

        lax.fori_loop(0, blocks, step, 0)


def attend(qkv, tile, lengths):
    blocks, count, width, block = qkv.shape
    heads = width // (3 * HD)
    total = blocks * block
    return pl.pallas_call(
        attend_kernel,
        grid=(count,),
        in_specs=[
            pl.BlockSpec(memory_space=pltpu.SMEM),
            pl.BlockSpec((blocks, 1, width, block), lambda i: (0, i, 0, 0)),
            pl.BlockSpec(tile.shape, lambda i: (0, 0, 0)),
        ],
        out_specs=[
            pl.BlockSpec((blocks, 1, heads * HD, block), lambda i: (0, i, 0, 0)),
            pl.BlockSpec((1, heads * blocks, block), lambda i: (i, 0, 0)),
        ],
        out_shape=[
            jax.ShapeDtypeStruct((blocks, count, heads * HD, block), BF16),
            jax.ShapeDtypeStruct((count, heads * blocks, block), F32),
        ],
        compiler_params=pltpu.CompilerParams(vmem_limit_bytes=VMEM_LIMIT),
        cost_estimate=pl.CostEstimate(
            flops=80 * count * heads * total * total * HD,
            bytes_accessed=2 * qkv.size + 4 * tile.size,
            transcendentals=count * heads * total * total,
        ),
        name="attend",
    )(lengths, qkv, tile)


def attend_back_kernel(
    length_ref, qkv_ref, out_grad_ref, lse_ref, tile_ref, grad_ref, rel_ref, sums_ref, dk_ref, dv_ref
):
    blocks, _, width, block = qkv_ref.shape
    total = blocks * block
    heads = width // (3 * HD)
    count = pl.num_programs(0)
    length = length_ref[pl.program_id(0)]
    scale = HD ** (-0.5)

    @pl.when(pl.program_id(0) == 0)
    def _():
        sums_ref[...] = jnp.zeros_like(sums_ref)

    for head in range(heads):
        at = head * HD
        key_t = head_columns(qkv_ref, 1, heads, head)
        key = key_t.T
        value = head_columns(qkv_ref, 2, heads, head).T
        dk_ref[...] = jnp.zeros_like(dk_ref)
        dv_ref[...] = jnp.zeros_like(dv_ref)

        def step(index, carried, head=head, at=at, key=key, key_t=key_t, value=value):
            query_t = qkv_ref[index, 0, at : at + HD, :]
            upstream_t = out_grad_ref[index, 0, at : at + HD, :]
            start = pl.multiple_of((blocks - 1 - index) * block, block)
            scores = transposed_scores(length, key, query_t, tile_ref, head, start, total)
            weights = jnp.exp(scores - lse_ref[0, pl.ds(head * blocks + index, 1), :])
            grad_weights = matmul(value, upstream_t)
            product = weights * grad_weights
            delta = jnp.sum(product, 0, keepdims=True)
            grad_scores = (product - weights * delta).astype(BF16)
            grad_ref[index, 0, at : at + HD, :] = (matmul(key_t, grad_scores) * scale).astype(BF16)
            dk_ref[...] += contract(query_t, grad_scores, 1, 1)
            dv_ref[...] += contract(upstream_t, weights.astype(BF16), 1, 1)
            sums_ref[head, pl.ds(start, total), :] += grad_scores.astype(F32)
            return carried

        lax.fori_loop(0, blocks, step, 0)
        key_at, value_at = heads * HD + at, 2 * heads * HD + at
        for index in range(blocks):
            columns = slice(index * block, (index + 1) * block)
            grad_ref[index, 0, key_at : key_at + HD, :] = (dk_ref[:, columns] * scale).astype(BF16)
            grad_ref[index, 0, value_at : value_at + HD, :] = dv_ref[:, columns].astype(BF16)

    @pl.when(pl.program_id(0) == count - 1)
    def _():
        length_all = 2 * total
        for head in range(heads):
            rows = jnp.concatenate([jnp.zeros((block, block), F32), sums_ref[head].T], 1)
            half = block // 2
            while half >= 8:
                rows = rows[:half] + pltpu.roll(rows[half:], length_all - half, 1)
                half //= 2
            folded = rows[:1]
            for row in range(1, 8):
                folded = folded + pltpu.roll(rows, length_all - row, 1)[row : row + 1]
            rel_ref[head] = folded


def attend_back(qkv, out_grad, lse, tile, lengths):
    blocks, count, width, block = qkv.shape
    heads = width // (3 * HD)
    total = blocks * block
    grads, rel = pl.pallas_call(
        attend_back_kernel,
        grid=(count,),
        in_specs=[
            pl.BlockSpec(memory_space=pltpu.SMEM),
            pl.BlockSpec((blocks, 1, width, block), lambda i: (0, i, 0, 0)),
            pl.BlockSpec((blocks, 1, heads * HD, block), lambda i: (0, i, 0, 0)),
            pl.BlockSpec((1, heads * blocks, block), lambda i: (i, 0, 0)),
            pl.BlockSpec(tile.shape, lambda i: (0, 0, 0)),
        ],
        out_specs=[
            pl.BlockSpec((blocks, 1, width, block), lambda i: (0, i, 0, 0)),
            pl.BlockSpec((heads, 1, 2 * total), lambda i: (0, 0, 0)),
        ],
        out_shape=[
            jax.ShapeDtypeStruct((blocks, count, width, block), BF16),
            jax.ShapeDtypeStruct((heads, 1, 2 * total), F32),
        ],
        scratch_shapes=[
            pltpu.VMEM(tile.shape, F32),
            pltpu.VMEM((HD, total), F32),
            pltpu.VMEM((HD, total), F32),
        ],
        compiler_params=pltpu.CompilerParams(vmem_limit_bytes=VMEM_LIMIT),
        cost_estimate=pl.CostEstimate(
            flops=125 * count * heads * total * total * HD,
            bytes_accessed=4 * qkv.size + 4 * tile.size,
            transcendentals=count * heads * total * total,
        ),
        name="attend_back",
    )(lengths, qkv, out_grad, lse, tile)
    return (grads, rel[:, 0, 1:])


def project_kernel(hidden_ref, gain_ref, weight_ref, out_ref, normed_ref, scale_ref):
    ways, _, width, _ = out_ref.shape
    normed, scale = rms_norm(hidden_ref[0], gain_ref[...])
    normed = normed.astype(BF16)
    normed_ref[0] = normed
    scale_ref[0] = scale
    for way in range(ways):
        columns = weight_ref[:, way * width : (way + 1) * width]
        out_ref[way, 0] = matmul(normed, columns).astype(BF16).T


def project(hidden, gain, dense, ways):
    count, rows, width = hidden.shape
    part = 3 * width // ways
    return pl.pallas_call(
        project_kernel,
        grid=(count,),
        in_specs=[
            pl.BlockSpec((1, rows, width), lambda i: (i, 0, 0)),
            pl.BlockSpec((1, width), lambda i: (0, 0)),
            pl.BlockSpec((width, 3 * width), lambda i: (0, 0)),
        ],
        out_specs=[
            pl.BlockSpec((ways, 1, part, rows), lambda i: (0, i, 0, 0)),
            pl.BlockSpec((1, rows, width), lambda i: (i, 0, 0)),
            pl.BlockSpec((1, rows, 1), lambda i: (i, 0, 0)),
        ],
        out_shape=[
            jax.ShapeDtypeStruct((ways, count, part, rows), BF16),
            jax.ShapeDtypeStruct((count, rows, width), BF16),
            jax.ShapeDtypeStruct((count, rows, 1), F32),
        ],
        compiler_params=pltpu.CompilerParams(vmem_limit_bytes=VMEM_LIMIT),
        cost_estimate=pl.CostEstimate(
            flops=6 * count * rows * width * width,
            bytes_accessed=12 * count * rows * width + 6 * width * width,
            transcendentals=0,
        ),
        name="project",
    )(hidden, gain[None], dense)


def embed_adam_kernel(rate, clip_ref, seq_ref, weight_ref, first_ref, second_ref, *refs):
    ways = len(refs) - 3
    held = [ref[...] for ref in refs[:ways]]
    ordered = []
    for source in range(ways):
        part = held[0]
        for distance in range(1, ways):
            part = jnp.where(seq_ref[0] == source ^ distance, held[distance], part)
        ordered.append(part.astype(F32).T)
    grad = jnp.concatenate(ordered, 1)
    updated = adam_update(
        weight_ref[...], grad * clip_ref[0], first_ref[...], second_ref[...], rate
    )
    for ref, value in zip(refs[ways:], updated):
        ref[...] = value


def embed_adam(weight, grads, first, second, clip, rate):
    rows, width = weight.shape
    block = min(256, rows)
    state = pl.BlockSpec((block, width), lambda i: (i, 0))
    return pl.pallas_call(
        functools.partial(embed_adam_kernel, rate),
        grid=(pl.cdiv(rows, block),),
        in_specs=[pl.BlockSpec(memory_space=pltpu.SMEM)] * 2
        + [state] * 3
        + [pl.BlockSpec((grads[0].shape[0], block), lambda i: (0, i))] * len(grads),
        out_specs=[state, state, state],
        out_shape=[jax.ShapeDtypeStruct((rows, width), F32)] * 3,
        compiler_params=pltpu.CompilerParams(vmem_limit_bytes=VMEM_LIMIT),
        cost_estimate=pl.CostEstimate(
            flops=20 * rows * width, bytes_accessed=26 * rows * width, transcendentals=rows * width
        ),
        name="embed_adam",
    )(clip.reshape(1), lax.axis_index("seq").reshape(1), weight, first, second, *grads)


def token_grad_kernel(ids_ref, *refs):
    *moved_refs, head_ref, out_ref, sums_ref = refs
    block = sums_ref.shape[0]

    @pl.when(pl.program_id(1) == 0)
    def _():
        sums_ref[...] = jnp.zeros_like(sums_ref)

    first = pl.program_id(0) * block
    for batch, moved_ref in enumerate(moved_refs):
        ids = ids_ref[0, batch : batch + 1, :]
        vocab = lax.broadcasted_iota(jnp.int32, (block, ids.shape[1]), 0) + first
        chosen = jnp.where(vocab == ids, 1.0, 0.0).astype(BF16)
        moved = jnp.concatenate([moved_ref[0, way] for way in range(moved_ref.shape[1])], 1)
        sums_ref[...] += contract(chosen, moved, 1, 1)

    @pl.when(pl.program_id(1) == pl.num_programs(1) - 1)
    def _():
        out_ref[...] = (sums_ref[...].T + head_ref[...]).astype(BF16)


def token_grad(ids, moved, head_grad):
    owners, count, tokens = ids.shape
    part, vocab_rows = head_grad.shape
    block = min(1024, -(-vocab_rows // 128) * 128)
    return pl.pallas_call(
        token_grad_kernel,
        grid=(pl.cdiv(vocab_rows, block), owners),
        in_specs=[pl.BlockSpec((1, count, tokens), lambda i, j: (j, 0, 0))]
        + [pl.BlockSpec((1,) + item.shape[1:], lambda i, j: (j, 0, 0, 0)) for item in moved]
        + [pl.BlockSpec((part, block), lambda i, j: (0, i))],
        out_specs=pl.BlockSpec((part, block), lambda i, j: (0, i)),
        out_shape=jax.ShapeDtypeStruct((part, vocab_rows), BF16),
        scratch_shapes=[pltpu.VMEM((block, part), F32)],
        compiler_params=pltpu.CompilerParams(vmem_limit_bytes=VMEM_LIMIT),
        cost_estimate=pl.CostEstimate(
            flops=4 * vocab_rows * owners * count * tokens * part,
            bytes_accessed=8 * owners * count * tokens * part,
            transcendentals=0,
        ),
        name="token_grad",
    )(ids, *moved, head_grad)


def exchange(parts):
    return lax.all_to_all(parts, "seq", split_axis=0, concat_axis=0, tiled=True)


def to_relative(part, distance):
    ways = lax.axis_size("seq")
    return lax.ppermute(part, "seq", [(way, way ^ distance) for way in range(ways)])


def share(part):
    return [part] + [to_relative(part, k) for k in range(1, lax.axis_size("seq"))]


def by_source(parts):
    seq_index = lax.axis_index("seq")
    first = parts[0]
    whole = jnp.zeros(first.shape[:1] + (len(parts),) + first.shape[1:], first.dtype)
    for distance, part in enumerate(parts):
        at = (0, seq_index ^ distance) + (0,) * (first.ndim - 1)
        whole = lax.dynamic_update_slice(whole, part[:, None], at)
    return whole


def sum_over_seq(parts):
    seq_index = lax.axis_index("seq")
    mine = lax.dynamic_index_in_dim(parts, seq_index, 0, False).astype(F32)
    for k in range(1, lax.axis_size("seq")):
        part = lax.dynamic_index_in_dim(parts, seq_index ^ k, 0, False)
        mine = mine + to_relative(part, k).astype(F32)
    return mine


def as_rows(flat):
    return jnp.pad(flat, (0, -flat.size % 1024)).reshape(-1, 128)


def sum_everywhere(parts):
    ways, owners = parts.shape[:2]
    size = parts.size // (ways * owners)
    flat = parts.reshape(ways * owners, size)
    flat = jnp.pad(flat, ((0, 0), (0, -size % 1024))).reshape(ways * owners, -1, 128)
    moved = lax.all_to_all(flat, ("seq", "fsdp"), split_axis=0, concat_axis=0, tiled=True)
    return jnp.sum(moved, 0).reshape(-1)[:size]


def after(value, *others):
    return lax.optimization_barrier((value,) + others)


def layer_forward(hidden, weights, gain_one, gain_two, router_w, tile, moe, lengths):
    dense, upward_w, downward_w = weights
    count, rows, width = hidden.shape
    output_w = dense[:, 3 * width :]
    ways = lax.axis_size("seq")
    dispatch, onehot = moe
    slots = dispatch.shape[1]
    projected, normed_one, scale_one = project(hidden, gain_one, dense, ways)
    qkv = exchange(projected)
    mixed, lse = attend(qkv, tile, lengths)
    mixed_t = exchange(mixed).reshape(width, rows)
    after_attn = hidden + contract(mixed_t, output_w, 0, 0).reshape(hidden.shape)
    normed_two, scale_two = rms_norm(after_attn, gain_two)
    normed_two = normed_two.astype(BF16)
    router_probs = jax.nn.softmax(
        matmul(normed_two.reshape(count * rows, width), router_w).reshape(count, rows, -1), -1
    )
    gate = jnp.sum(router_probs * onehot, -1, keepdims=True)
    sent = jnp.einsum("nst,ntd->nsd", dispatch, normed_two, preferred_element_type=F32).astype(BF16)
    sent = sent.reshape(count, ways, slots // ways, width).transpose(1, 0, 2, 3)
    expert_rows = exchange(sent).reshape(count * slots, width)
    upward = matmul(expert_rows, upward_w)
    activated = jax.nn.gelu(upward).astype(BF16)
    expert_out = matmul(activated, downward_w).astype(BF16)
    back = exchange(expert_out.reshape(ways, count, slots // ways, width))
    back = back.transpose(1, 0, 2, 3).reshape(count, slots, width)
    token_out = jnp.einsum("nst,nsd->ntd", dispatch, back, preferred_element_type=F32)
    result = after_attn + gate * token_out
    kept = dict(
        hidden=hidden,
        scale_one=scale_one,
        normed_one=normed_one,
        qkv=qkv,
        lse=lse,
        mixed_t=mixed_t,
        after_attn=after_attn,
        mixed=mixed,
        scale_two=scale_two,
        normed_two=normed_two,
        router_probs=router_probs,
        gate=gate,
        expert_rows=expert_rows,
        upward=upward,
        activated=activated,
        token_out=token_out,
    )
    return (result, kept)


def experts_backward(grad_out, kept, weights, moe):
    _, upward_w, downward_w = weights
    count, rows, width = grad_out.shape
    ways = lax.axis_size("seq")
    dispatch, _ = moe
    slots = dispatch.shape[1]
    grad_token = (kept["gate"] * grad_out).astype(BF16)
    sent = jnp.einsum("nst,ntd->nsd", dispatch, grad_token, preferred_element_type=F32).astype(BF16)
    sent = sent.reshape(count, ways, slots // ways, width).transpose(1, 0, 2, 3)
    grad_expert = exchange(sent).reshape(count * slots, width)
    grad_activated = contract(grad_expert, downward_w, 1, 1)
    grad_upward = jax.vjp(jax.nn.gelu, kept["upward"])[1](grad_activated)[0].astype(BF16)
    grad_rows = contract(grad_upward, upward_w, 1, 1).astype(BF16)
    back = exchange(grad_rows.reshape(ways, count, slots // ways, width))
    return (back, ((kept["expert_rows"], grad_upward), (kept["activated"], grad_expert)))


def mixed_backward(grad_out, back, kept, weights, gain_two, router_w, moe):
    dense, _, _ = weights
    count, rows, width = grad_out.shape
    output_w = dense[:, 3 * width :]
    ways = lax.axis_size("seq")
    dispatch, onehot = moe
    slots = dispatch.shape[1]
    flat = (count * rows, width)
    grad_gate = jnp.sum(grad_out * kept["token_out"], -1, keepdims=True)
    back = back.transpose(1, 0, 2, 3).reshape(count, slots, width)
    grad_normed = jnp.einsum("nst,nsd->ntd", dispatch, back, preferred_element_type=F32)
    grad_probs = onehot * grad_gate
    router_probs = kept["router_probs"]
    grad_logits = (
        router_probs * (grad_probs - jnp.sum(grad_probs * router_probs, -1, keepdims=True))
    ).astype(BF16)
    grad_logits = grad_logits.reshape(count * rows, -1)
    grad_router = contract(kept["normed_two"].reshape(flat), grad_logits, 0, 0)
    grad_normed = grad_normed.reshape(flat) + contract(grad_logits, router_w, 1, 1)
    grad_mid, grad_gain_two = rms_back(
        kept["after_attn"].reshape(flat), kept["scale_two"].reshape(-1, 1), gain_two, grad_normed
    )
    grad_mid = grad_mid + grad_out.reshape(flat)
    grad_attn = grad_mid.astype(BF16)
    grad_mixed_t = contract(output_w, grad_attn, 1, 1).astype(BF16)
    grad_mixed_t = exchange(grad_mixed_t.reshape(ways, 1, width // ways, rows))
    return (grad_mixed_t, grad_mid, (kept["mixed_t"], grad_attn), (grad_gain_two, grad_router))


def attention_backward(grad_mixed_t, grad_mid, kept, weights, gain_one, tile, lengths, piece):
    dense, _, _ = weights
    count, rows, width = kept["hidden"].shape
    attend_w = dense[:, : 3 * width]
    flat = (count * rows, width)
    grad_mixed_t, piece = after(grad_mixed_t, piece)
    grad_qkv, grad_relative = attend_back(kept["qkv"], grad_mixed_t, kept["lse"], tile, lengths)
    grad_qkv, piece = after(grad_qkv, sum_over_seq(piece))
    grad_projected_t = exchange(grad_qkv).reshape(3 * width, rows)
    grad_first, grad_gain_one = rms_back(
        kept["hidden"].reshape(flat),
        kept["scale_one"].reshape(-1, 1),
        gain_one,
        contract(grad_projected_t, attend_w, 0, 1),
    )
    return (
        (grad_mid + grad_first).reshape(count, rows, width),
        (kept["normed_one"].reshape(flat), grad_projected_t),
        (grad_gain_one, grad_relative),
        piece,
    )


def weight_grad(pairs, left_dim, right_dim):
    return contract(
        jnp.concatenate([item[0] for item in pairs], left_dim),
        jnp.concatenate([item[1] for item in pairs], right_dim),
        left_dim,
        right_dim,
    ).astype(BF16)


def adam_update(weight, grad, first, second, rate):
    first = BETA_ONE * first + (1.0 - BETA_ONE) * grad
    second = BETA_TWO * second + (1.0 - BETA_TWO) * grad * grad
    mean_hat = first / (1.0 - BETA_ONE**STEP_COUNT)
    square_hat = second / (1.0 - BETA_TWO**STEP_COUNT)
    weight = weight - rate * (
        mean_hat / (jnp.sqrt(square_hat) + ADAM_EPSILON) + WEIGHT_DECAY * weight
    )
    return (weight, first, second)


def scatter_owners(item):
    return lax.psum_scatter(item, "fsdp", scatter_dimension=0, tiled=True)


def sum_squares(*arrays):
    return sum(jnp.sum(jnp.square(item.astype(F32))) for item in arrays)


def per_device(
    token_ids,
    lengths,
    routes,
    positions,
    targets,
    teacher_index,
    teacher_weight,
    buckets,
    embed_weight,
    embed_mean,
    embed_square,
    attend_weight,
    attend_mean,
    attend_square,
    output_weight,
    output_mean,
    output_square,
    upward_weight,
    upward_mean,
    upward_square,
    downward_weight,
    downward_mean,
    downward_square,
    router_weight,
    router_mean,
    router_square,
    gains_weight,
    gains_mean,
    gains_square,
    bias_weight,
    bias_mean,
    bias_square,
):
    ways, owners = lax.axis_size("seq"), lax.axis_size("fsdp")
    seq_index, owner_index = lax.axis_index("seq"), lax.axis_index("fsdp")
    layers, experts = upward_weight.shape[0], upward_weight.shape[1]
    vocab_rows, width = embed_weight.shape
    count, rows = token_ids.shape[0], token_ids.shape[2]
    total = rows * ways
    picks = positions.shape[2]
    shard = upward_weight.shape[2]
    part = width // ways
    capacity = rows * 3 // 8
    factor = width ** (-0.5)
    lengths = lengths[:, 0]

    def dense_shard(layer):
        attend_low = attend_weight[layer].reshape(shard, 3, ways, part).transpose(0, 2, 1, 3)
        return jnp.concatenate(
            [attend_low.reshape(shard, 3 * width).astype(BF16), output_weight[layer].astype(BF16)], 1
        )

    def gather_owners(item):
        return lax.all_gather(item, "fsdp", axis=0, tiled=True)

    def gather_expert(item, layer):
        mine = lax.dynamic_index_in_dim(item[layer], seq_index, 0, False)
        return gather_owners(mine.astype(BF16))

    first_dense = dense_shard(0)
    own_ids, first_dense = after(token_ids[:, 0], first_dense)
    first_dense = gather_owners(first_dense)
    group_ids = lax.all_gather(own_ids, "fsdp", axis=0, tiled=False)
    valid_own = (seq_index * rows + positions[:, 0] < lengths[:, None]).astype(F32)
    teacher_own = teacher_weight[:, 0] / jnp.sum(teacher_weight[:, 0], -1, keepdims=True)
    small = jnp.concatenate(
        [
            lax.optimization_barrier(item.astype(BF16)).astype(F32).reshape(-1)
            for item in (gains_weight, bias_weight, router_weight)
        ]
        + [item.astype(F32).reshape(-1) for item in (valid_own, targets, teacher_index, teacher_own)]
    )
    small = lax.all_gather(as_rows(small), "fsdp", axis=0, tiled=False)
    embed_low = embed_weight.astype(BF16)
    vocab_ids = jnp.arange(vocab_rows)
    founds = []
    for batch in range(count):
        local_ids = group_ids[:, batch].reshape(-1) - owner_index * vocab_rows
        if batch == count - 1:
            local_ids, small = after(local_ids, small)
        founds.append(
            matmul((local_ids[:, None] == vocab_ids[None, :]).astype(BF16), embed_low).astype(BF16)
        )
        if batch == count - 1:
            founds[-1], first_dense = after(founds[-1], first_dense)
    later = (attend_weight, output_weight, upward_weight, downward_weight)
    founds[-1], *later = after(founds[-1], *later)
    hiddens = [
        lax.psum_scatter(
            found.reshape(owners, rows, width), "fsdp", scatter_dimension=0, tiled=False
        )
        .astype(F32)
        .reshape(1, rows, width)
        for found in founds
    ]
    weights = []
    for layer in range(layers):
        weights.append(
            (
                gather_owners(dense_shard(layer)) if layer else first_dense,
                gather_expert(later[2], layer),
                gather_expert(later[3], layer),
            )
        )

    small = small.reshape(owners, -1)
    pieces, at = [], 0
    for item in (gains_weight, bias_weight, router_weight, valid_own, targets, teacher_index, teacher_own):
        pieces.append(small[:, at : at + item.size])
        at += item.size
    norms = 2 * layers + 1
    gains_full = pieces[0].reshape(owners, norms, shard).transpose(1, 0, 2).reshape(norms, width)
    bias_full = pieces[1].reshape(owners, layers, -1).transpose(1, 0, 2).reshape(layers, -1, H)
    router_full = (
        pieces[2].reshape(owners, layers, shard, experts).transpose(1, 0, 2, 3).astype(BF16)
    ).reshape(layers, width, experts)
    valid_all = pieces[3].reshape(-1)
    targets_all = pieces[4].astype(jnp.int32).reshape(-1, 1)
    index_all = pieces[5].astype(jnp.int32).reshape(-1, teacher_index.shape[3])
    teacher_all = pieces[6].reshape(-1, teacher_index.shape[3])

    head_local = H // ways
    local_tables = lax.dynamic_slice_in_dim(bias_full, seq_index * head_local, head_local, 2)
    onehot_buckets = (buckets[:, None] == jnp.arange(bias_full.shape[1])[None, :]).astype(F32)
    tiles = [
        bias_tile(
            jnp.dot(onehot_buckets, local_tables[layer], precision=HIGHEST_PRECISION).T, rows, total
        )
        for layer in range(layers)
    ]

    route_ids = routes[:, 0, :, 0]
    onehot = (route_ids[..., None] == jnp.arange(experts)).astype(F32)
    ranks = jnp.sum((jnp.cumsum(onehot, 1) - 1.0) * onehot, -1).astype(jnp.int32)
    slot_index = route_ids * capacity + ranks
    dispatch = (slot_index[:, None, :] == jnp.arange(experts * capacity)[None, :, None]).astype(BF16)

    base = owner_index * vocab_rows
    entry = jnp.concatenate([index_all, targets_all], 1) - base
    mass = jnp.concatenate([teacher_all, jnp.ones_like(teacher_all[:, :1])], 1)
    lanes = 128
    groups = -(-vocab_rows // lanes)
    entry = jnp.where((entry >= 0) & (entry < vocab_rows), entry, groups * lanes)
    high = (entry[..., None] // lanes == jnp.arange(groups)).astype(F32) * mass[..., None]
    low = (entry[..., None] % lanes == jnp.arange(lanes)).astype(F32)
    wanted = jnp.einsum("rkh,rkl->rhl", high, low, precision=HIGHEST_PRECISION)
    wanted = wanted.reshape(-1, groups * lanes)[:, :vocab_rows]
    mass_all = jnp.sum(teacher_all, -1, keepdims=True) + 1.0

    kept_all = [[None] * count for layer in range(layers)]
    moes = [(dispatch[batch : batch + 1], onehot[batch : batch + 1]) for batch in range(count)]
    used = [lengths[batch : batch + 1] for batch in range(count)]
    for layer in range(layers):
        for batch in range(count):
            if layer == 0 and batch:
                hiddens[batch], wanted, _ = after(hiddens[batch], wanted, kept_all[0][batch - 1]["mixed"])
            hiddens[batch], kept_all[layer][batch] = layer_forward(
                hiddens[batch],
                weights[layer],
                gains_full[2 * layer],
                gains_full[2 * layer + 1],
                router_full[layer],
                tiles[layer],
                moes[batch],
                used[batch],
            )
        if layer == 0:
            every_id = lax.all_gather(group_ids, "seq", axis=0, tiled=False) - owner_index * vocab_rows
            every_id = every_id.transpose(1, 2, 0, 3).reshape(owners, count, -1)
            hiddens[-1], every_id = after(hiddens[-1], every_id)
    hidden = jnp.concatenate(hiddens, 0)

    final, scale_final = rms_norm(hidden, gains_full[2 * layers])
    chosen = (positions[:, 0][..., None] == jnp.arange(rows)).astype(BF16)
    picked = jnp.einsum("npt,ntd->npd", chosen, final.astype(BF16), preferred_element_type=F32)
    picked = lax.all_gather(
        picked.astype(BF16).reshape(count * picks, width), "fsdp", axis=0, tiled=True
    )
    logits = contract(picked, embed_low, 1, 1) * factor
    peak = jnp.max(logits, -1)
    stats = jnp.stack([peak, jnp.sum(jnp.exp(logits - peak[:, None]), -1)])
    stats = lax.all_gather(stats, "fsdp", axis=0, tiled=False)
    peak_all = jnp.max(stats[:, 0], 0)
    lse_all = peak_all + jnp.log(jnp.sum(stats[:, 1] * jnp.exp(stats[:, 0] - peak_all), 0))
    grad_logits = mass_all * jnp.exp(logits - lse_all[:, None]) - wanted
    grad_logits = (grad_logits * valid_all[:, None]).astype(BF16)
    lse_own = lax.dynamic_slice_in_dim(lse_all, owner_index * count * picks, count * picks, 0)
    mass_own = jnp.sum(teacher_own, -1) + 1.0
    own_rows = jnp.sum(teacher_own * jnp.log(teacher_own), -1) + mass_own * lse_own.reshape(count, picks)
    loss_part = jnp.sum(valid_own * own_rows) - jnp.sum(
        valid_all * jnp.sum(wanted * logits, -1)
    )
    grad_picked = lax.psum_scatter(
        matmul(grad_logits, embed_low), "fsdp", scatter_dimension=0, tiled=True
    )
    grad_picked = (grad_picked * factor).reshape(count, picks, width)
    head_grad = (matmul(lax.optimization_barrier(picked.T), grad_logits) * factor).astype(BF16)
    head_grad = head_grad.reshape(ways, part, vocab_rows)
    run = -(-vocab_rows // (128 * layers * count)) * 128
    pieces = [head_grad[:, :, at : at + run] for at in range(0, vocab_rows, run)]
    pieces += [None] * (layers * count - len(pieces))
    summed = []
    grad_final = jnp.einsum(
        "npt,npd->ntd", chosen.astype(F32), grad_picked, precision=HIGHEST_PRECISION
    )
    grad_hidden, grad_gain_final = rms_back(
        hidden.reshape(count * rows, width),
        scale_final.reshape(-1, 1),
        gains_full[2 * layers],
        grad_final.reshape(count * rows, width),
    )
    grad_hidden = grad_hidden.reshape(hidden.shape)
    grad_hiddens = [grad_hidden[batch : batch + 1] for batch in range(count)]

    gain_grads = [None] * norms
    gain_grads[2 * layers] = grad_gain_final
    router_grads, table_grads = [None] * layers, [None] * layers
    grad_parts = [None] * layers
    for layer in reversed(range(layers)):
        one, two = 2 * layer, 2 * layer + 1
        stages, passed = [None] * count, grad_parts[layer + 1] if layer + 1 < layers else None
        for batch in range(count):
            back, pairs = experts_backward(
                grad_hiddens[batch], kept_all[layer][batch], weights[layer], moes[batch]
            )
            if passed and batch < 2:
                back, passed[batch] = after(back, passed[batch])
            stages[batch] = (back, pairs)
        up_down = [
            weight_grad([pairs[which] for _, pairs in stages], 0, 0) for which in range(2)
        ]
        grad_parts[layer] = [scatter_owners(item) for item in up_down]
        outer, smalls = [], []
        for batch in range(count):
            grad_mixed_t, grad_mid, pair, small_two = mixed_backward(
                grad_hiddens[batch],
                stages[batch][0],
                kept_all[layer][batch],
                weights[layer],
                gains_full[two],
                router_full[layer],
                moes[batch],
            )
            if batch == count - 1:
                grad_mixed_t, *up_down = after(grad_mixed_t, *up_down)
                if passed:
                    grad_mixed_t, passed[2] = after(grad_mixed_t, passed[2])
                if layer == 0:
                    grad_mixed_t, grad_parts[0][0] = after(grad_mixed_t, grad_parts[0][0])
            grad_hiddens[batch], attend_pair, small_one, piece = attention_backward(
                grad_mixed_t,
                grad_mid,
                kept_all[layer][batch],
                weights[layer],
                gains_full[one],
                tiles[layer],
                used[batch],
                pieces[len(summed)],
            )
            summed.append(piece)
            outer.append((attend_pair, pair))
            smalls.append(small_one + small_two)
        gain_grads[one], grad_relative, gain_grads[two], router_grads[layer] = (
            sum(items) for items in zip(*smalls)
        )
        table_grads[layer] = jnp.dot(onehot_buckets.T, grad_relative.T, precision=HIGHEST_PRECISION)
        dense_grad = jnp.concatenate(
            [weight_grad([item[0] for item in outer], 0, 1), weight_grad([item[1] for item in outer], 1, 0)],
            1,
        )
        if layer:
            grad_hiddens[0], dense_grad = after(grad_hiddens[0], dense_grad)
            grad_parts[layer].append(scatter_owners(dense_grad))

    moved = []
    for batch in range(count):
        columns = grad_hiddens[batch].reshape(rows, width).astype(BF16).T
        moved.append(exchange(columns.reshape(ways, part, rows)))
    moved[-1], grad_parts[0][1] = after(moved[-1], grad_parts[0][1])
    stacks = [jnp.stack([parts[which] for parts in grad_parts]) for which in range(2)]
    moved[-1], dense_grad, *stacks = after(moved[-1], dense_grad, *stacks)
    moved[0], dense_grad = after(moved[0], dense_grad)
    moved = [lax.all_gather(item, "fsdp", axis=0, tiled=False) for item in moved]
    grad_parts[0].append(scatter_owners(dense_grad))
    head_grad = jnp.concatenate([piece for piece in summed if piece is not None], 1)
    wholes = [share(item) for item in stacks]
    embed_part = token_grad(every_id, moved, head_grad)
    dense = jnp.stack([parts[2] for parts in grad_parts])
    dense = jnp.concatenate(
        [
            dense[:, :, : 3 * width].reshape(layers, shard, ways, 3 * part),
            dense[:, :, 3 * width :].reshape(layers, shard, ways, part),
        ],
        3,
    )
    dense_part = sum_over_seq(dense.transpose(2, 0, 1, 3)).astype(BF16)

    tables = lax.dynamic_update_slice(
        jnp.zeros(bias_full.shape, F32), jnp.stack(table_grads), (0, 0, seq_index * head_local)
    )
    bias_shard = bias_weight.shape[1]
    tiny = jnp.concatenate(
        [
            jnp.stack(gain_grads).reshape(norms, owners, shard).transpose(1, 0, 2).reshape(owners, -1),
            tables.reshape(layers, owners, bias_shard).transpose(1, 0, 2).reshape(owners, -1),
            jnp.stack(router_grads)
            .reshape(layers, owners, shard, experts)
            .transpose(1, 0, 2, 3)
            .reshape(owners, -1),
            jnp.broadcast_to(jnp.stack([loss_part, jnp.sum(valid_own)])[None], (owners, 2)),
        ],
        1,
    )
    tiny = sum_everywhere(jnp.broadcast_to(tiny[None], (ways,) + tiny.shape))
    gain_size, bias_size = gains_weight.size, bias_weight.size
    gains_grad = tiny[:gain_size].reshape(gains_weight.shape)
    bias_grad = tiny[gain_size : gain_size + bias_size].reshape(bias_weight.shape)
    router_grad = tiny[gain_size + bias_size : -2].reshape(router_weight.shape)
    loss_value, loss_count = tiny[-2], tiny[-1]

    squares_part = (
        sum_squares(embed_part, dense_part, *stacks)
        + sum_squares(gains_grad, bias_grad, router_grad) / ways
    )
    grad_norm = jnp.sqrt(
        sum_everywhere(jnp.broadcast_to(squares_part, (ways, owners, 1)))[0]
    )
    clip_factor = jnp.minimum(1.0, CLIP_NORM / (grad_norm + 1e-06))

    embed_grads = share(embed_part)
    upward_grad, downward_grad = (by_source(items) for items in wholes)
    dense_grad = by_source(share(dense_part)).transpose(0, 2, 1, 3)
    attend_grad = dense_grad[..., : 3 * part].reshape(layers, shard, ways, 3, part)
    attend_grad = attend_grad.transpose(0, 1, 3, 2, 4).reshape(layers, shard, 3 * width)
    output_grad = dense_grad[..., 3 * part :].reshape(layers, shard, width)
    grads = (
        None,
        attend_grad,
        output_grad,
        upward_grad,
        downward_grad,
        router_grad,
        gains_grad,
        bias_grad,
    )
    params = (
        embed_weight,
        attend_weight,
        output_weight,
        upward_weight,
        downward_weight,
        router_weight,
        gains_weight,
        bias_weight,
    )
    means = (
        embed_mean,
        attend_mean,
        output_mean,
        upward_mean,
        downward_mean,
        router_mean,
        gains_mean,
        bias_mean,
    )
    squares = (
        embed_square,
        attend_square,
        output_square,
        upward_square,
        downward_square,
        router_square,
        gains_square,
        bias_square,
    )
    results = [loss_value, loss_count, grad_norm]
    results.extend(
        embed_adam(embed_weight, embed_grads, embed_mean, embed_square, clip_factor, STEP_RATES[0])
    )
    for weight, grad, first, second, rate in list(
        zip(params, grads, means, squares, STEP_RATES)
    )[1:]:
        results.extend(adam_update(weight, grad.astype(F32) * clip_factor, first, second, rate))
    return tuple(results)


def solution(mesh):
    token = P(None, "fsdp", "seq")
    entry = P(None, "fsdp", "seq", None)
    state = (
        [P("fsdp", None)] * 3
        + [P(None, "fsdp", None)] * 6
        + [P(None, None, "fsdp", None)] * 6
        + [P(None, "fsdp", None)] * 3
        + [P(None, "fsdp")] * 6
    )
    return jax.shard_map(
        per_device,
        mesh=mesh,
        in_specs=tuple([token, P(None, "fsdp"), entry, token, token, entry, entry, P()] + state),
        out_specs=tuple([P(), P(), P()] + state),
        check_vma=False,
    )
```

```python
import functools

import jax
import jax.numpy as jnp
from jax import lax
from jax.experimental import pallas as pl
from jax.experimental.pallas import tpu as pltpu
from jax.sharding import PartitionSpec as P

H = 12
HD = 64
STEP_COUNT = 10

EPSILON = 1e-06
ADAM_EPSILON = 1e-08
BETA_ONE = 0.9
BETA_TWO = 0.999
WEIGHT_DECAY = 0.01
CLIP_NORM = 1.0
STEP_RATES = (0.5, 0.03, 0.3, 0.03, 0.04, 0.02, 0.9, 0.5)
HIGHEST_PRECISION = lax.Precision.HIGHEST
VMEM_LIMIT = 48 * 1024 * 1024
BF16 = jnp.bfloat16
F32 = jnp.float32


def matmul(left_side, right_side):
    return jnp.dot(left_side, right_side, preferred_element_type=F32)


def contract(left_side, right_side, left_dim, right_dim):
    return lax.dot_general(
        left_side,
        right_side,
        (((left_dim,), (right_dim,)), ((), ())),
        preferred_element_type=F32,
    )


def rms_norm(hidden, gain):
    norm_scale = lax.rsqrt(jnp.mean(hidden * hidden, -1, keepdims=True) + EPSILON)
    return (hidden * norm_scale * gain, norm_scale)


def rms_back(hidden, norm_scale, gain, upstream):
    normed = hidden * norm_scale
    grad_normed = upstream * gain
    grad_gain = jnp.sum(upstream * normed, 0)
    grad_hidden = norm_scale * (
        grad_normed - normed * jnp.mean(grad_normed * normed, -1, keepdims=True)
    )
    return (grad_hidden, grad_gain)


def bias_tile_kernel(rel_ref, tile_ref):
    heads, width, block = tile_ref.shape
    length = rel_ref.shape[2]
    for head in range(heads):
        spread = jnp.broadcast_to(rel_ref[head], (block, length))
        skewed = pltpu.roll(spread, length - (block - 1), 1, stride=1, stride_axis=0)
        tile_ref[head] = skewed[:, :width].T


def bias_tile(relative, block, total):
    heads, length = relative.shape
    width = 2 * total - block
    padded = jnp.pad(relative, ((0, 0), (0, 2 * total - length)))[:, None, :]
    return pl.pallas_call(
        bias_tile_kernel,
        out_shape=jax.ShapeDtypeStruct((heads, width, block), F32),
        compiler_params=pltpu.CompilerParams(vmem_limit_bytes=VMEM_LIMIT),
        name="bias_tile",
    )(padded)


def head_columns(ref, part, heads, head):
    at = (part * heads + head) * HD
    return jnp.concatenate([ref[index, 0, at : at + HD, :] for index in range(ref.shape[0])], 1)


def transposed_scores(length, key, query_t, tile_ref, head, start, total):
    scores = matmul(key, query_t) * HD ** (-0.5) + tile_ref[head, pl.ds(start, total), :]
    key_ids = lax.broadcasted_iota(jnp.int32, scores.shape, 0)
    return jnp.where(key_ids < length, scores, -1e30)


def attend_kernel(length_ref, qkv_ref, tile_ref, out_ref, lse_ref):
    blocks, _, width, block = qkv_ref.shape
    total = blocks * block
    heads = width // (3 * HD)
    length = length_ref[pl.program_id(0)]
    for head in range(heads):
        at = head * HD
        key = head_columns(qkv_ref, 1, heads, head).T
        value_t = head_columns(qkv_ref, 2, heads, head)

        def step(index, carried, head=head, at=at, key=key, value_t=value_t):
            query_t = qkv_ref[index, 0, at : at + HD, :]
            start = pl.multiple_of((blocks - 1 - index) * block, block)
            scores = transposed_scores(length, key, query_t, tile_ref, head, start, total)
            peak = jnp.max(scores, 0, keepdims=True)
            powers = jnp.exp(scores - peak)
            norm = jnp.sum(powers, 0, keepdims=True)
            weights = (powers * (1.0 / norm)).astype(BF16)
            out_ref[index, 0, at : at + HD, :] = matmul(value_t, weights).astype(BF16)
            lse_ref[0, pl.ds(head * blocks + index, 1), :] = peak + jnp.log(norm)
            return carried

        lax.fori_loop(0, blocks, step, 0)


def attend(qkv, tile, lengths):
    blocks, count, width, block = qkv.shape
    heads = width // (3 * HD)
    total = blocks * block
    return pl.pallas_call(
        attend_kernel,
        grid=(count,),
        in_specs=[
            pl.BlockSpec(memory_space=pltpu.SMEM),
            pl.BlockSpec((blocks, 1, width, block), lambda i: (0, i, 0, 0)),
            pl.BlockSpec(tile.shape, lambda i: (0, 0, 0)),
        ],
        out_specs=[
            pl.BlockSpec((blocks, 1, heads * HD, block), lambda i: (0, i, 0, 0)),
            pl.BlockSpec((1, heads * blocks, block), lambda i: (i, 0, 0)),
        ],
        out_shape=[
            jax.ShapeDtypeStruct((blocks, count, heads * HD, block), BF16),
            jax.ShapeDtypeStruct((count, heads * blocks, block), F32),
        ],
        compiler_params=pltpu.CompilerParams(vmem_limit_bytes=VMEM_LIMIT),
        cost_estimate=pl.CostEstimate(
            flops=80 * count * heads * total * total * HD,
            bytes_accessed=2 * qkv.size + 4 * tile.size,
            transcendentals=count * heads * total * total,
        ),
        name="attend",
    )(lengths, qkv, tile)


def attend_back_kernel(
    length_ref, qkv_ref, out_grad_ref, lse_ref, tile_ref, grad_ref, rel_ref, sums_ref, dk_ref, dv_ref
):
    blocks, _, width, block = qkv_ref.shape
    total = blocks * block
    heads = width // (3 * HD)
    count = pl.num_programs(0)
    length = length_ref[pl.program_id(0)]
    scale = HD ** (-0.5)

    @pl.when(pl.program_id(0) == 0)
    def _():
        sums_ref[...] = jnp.zeros_like(sums_ref)

    for head in range(heads):
        at = head * HD
        key_t = head_columns(qkv_ref, 1, heads, head)
        key = key_t.T
        value = head_columns(qkv_ref, 2, heads, head).T
        dk_ref[...] = jnp.zeros_like(dk_ref)
        dv_ref[...] = jnp.zeros_like(dv_ref)

        def step(index, carried, head=head, at=at, key=key, key_t=key_t, value=value):
            query_t = qkv_ref[index, 0, at : at + HD, :]
            upstream_t = out_grad_ref[index, 0, at : at + HD, :]
            start = pl.multiple_of((blocks - 1 - index) * block, block)
            scores = transposed_scores(length, key, query_t, tile_ref, head, start, total)
            weights = jnp.exp(scores - lse_ref[0, pl.ds(head * blocks + index, 1), :])
            grad_weights = matmul(value, upstream_t)
            product = weights * grad_weights
            delta = jnp.sum(product, 0, keepdims=True)
            grad_scores = (product - weights * delta).astype(BF16)
            grad_ref[index, 0, at : at + HD, :] = (matmul(key_t, grad_scores) * scale).astype(BF16)
            dk_ref[...] += contract(query_t, grad_scores, 1, 1)
            dv_ref[...] += contract(upstream_t, weights.astype(BF16), 1, 1)
            sums_ref[head, pl.ds(start, total), :] += grad_scores.astype(F32)
            return carried

        lax.fori_loop(0, blocks, step, 0)
        key_at, value_at = heads * HD + at, 2 * heads * HD + at
        for index in range(blocks):
            columns = slice(index * block, (index + 1) * block)
            grad_ref[index, 0, key_at : key_at + HD, :] = (dk_ref[:, columns] * scale).astype(BF16)
            grad_ref[index, 0, value_at : value_at + HD, :] = dv_ref[:, columns].astype(BF16)

    @pl.when(pl.program_id(0) == count - 1)
    def _():
        length_all = 2 * total
        for head in range(heads):
            rows = jnp.concatenate([jnp.zeros((block, block), F32), sums_ref[head].T], 1)
            half = block // 2
            while half >= 8:
                rows = rows[:half] + pltpu.roll(rows[half:], length_all - half, 1)
                half //= 2
            folded = rows[:1]
            for row in range(1, 8):
                folded = folded + pltpu.roll(rows, length_all - row, 1)[row : row + 1]
            rel_ref[head] = folded


def attend_back(qkv, out_grad, lse, tile, lengths):
    blocks, count, width, block = qkv.shape
    heads = width // (3 * HD)
    total = blocks * block
    grads, rel = pl.pallas_call(
        attend_back_kernel,
        grid=(count,),
        in_specs=[
            pl.BlockSpec(memory_space=pltpu.SMEM),
            pl.BlockSpec((blocks, 1, width, block), lambda i: (0, i, 0, 0)),
            pl.BlockSpec((blocks, 1, heads * HD, block), lambda i: (0, i, 0, 0)),
            pl.BlockSpec((1, heads * blocks, block), lambda i: (i, 0, 0)),
            pl.BlockSpec(tile.shape, lambda i: (0, 0, 0)),
        ],
        out_specs=[
            pl.BlockSpec((blocks, 1, width, block), lambda i: (0, i, 0, 0)),
            pl.BlockSpec((heads, 1, 2 * total), lambda i: (0, 0, 0)),
        ],
        out_shape=[
            jax.ShapeDtypeStruct((blocks, count, width, block), BF16),
            jax.ShapeDtypeStruct((heads, 1, 2 * total), F32),
        ],
        scratch_shapes=[
            pltpu.VMEM(tile.shape, F32),
            pltpu.VMEM((HD, total), F32),
            pltpu.VMEM((HD, total), F32),
        ],
        compiler_params=pltpu.CompilerParams(vmem_limit_bytes=VMEM_LIMIT),
        cost_estimate=pl.CostEstimate(
            flops=125 * count * heads * total * total * HD,
            bytes_accessed=4 * qkv.size + 4 * tile.size,
            transcendentals=count * heads * total * total,
        ),
        name="attend_back",
    )(lengths, qkv, out_grad, lse, tile)
    return (grads, rel[:, 0, 1:])


def project_kernel(hidden_ref, gain_ref, weight_ref, out_ref, normed_ref, scale_ref):
    ways, _, width, _ = out_ref.shape
    normed, scale = rms_norm(hidden_ref[0], gain_ref[...])
    normed = normed.astype(BF16)
    normed_ref[0] = normed
    scale_ref[0] = scale
    for way in range(ways):
        columns = weight_ref[:, way * width : (way + 1) * width]
        out_ref[way, 0] = matmul(normed, columns).astype(BF16).T


def project(hidden, gain, dense, ways):
    count, rows, width = hidden.shape
    part = 3 * width // ways
    return pl.pallas_call(
        project_kernel,
        grid=(count,),
        in_specs=[
            pl.BlockSpec((1, rows, width), lambda i: (i, 0, 0)),
            pl.BlockSpec((1, width), lambda i: (0, 0)),
            pl.BlockSpec((width, 3 * width), lambda i: (0, 0)),
        ],
        out_specs=[
            pl.BlockSpec((ways, 1, part, rows), lambda i: (0, i, 0, 0)),
            pl.BlockSpec((1, rows, width), lambda i: (i, 0, 0)),
            pl.BlockSpec((1, rows, 1), lambda i: (i, 0, 0)),
        ],
        out_shape=[
            jax.ShapeDtypeStruct((ways, count, part, rows), BF16),
            jax.ShapeDtypeStruct((count, rows, width), BF16),
            jax.ShapeDtypeStruct((count, rows, 1), F32),
        ],
        compiler_params=pltpu.CompilerParams(vmem_limit_bytes=VMEM_LIMIT),
        cost_estimate=pl.CostEstimate(
            flops=6 * count * rows * width * width,
            bytes_accessed=12 * count * rows * width + 6 * width * width,
            transcendentals=0,
        ),
        name="project",
    )(hidden, gain[None], dense)


def embed_adam_kernel(rate, clip_ref, seq_ref, weight_ref, first_ref, second_ref, *refs):
    ways = len(refs) - 3
    held = [ref[...] for ref in refs[:ways]]
    ordered = []
    for source in range(ways):
        part = held[0]
        for distance in range(1, ways):
            part = jnp.where(seq_ref[0] == source ^ distance, held[distance], part)
        ordered.append(part.astype(F32).T)
    grad = jnp.concatenate(ordered, 1)
    updated = adam_update(
        weight_ref[...], grad * clip_ref[0], first_ref[...], second_ref[...], rate
    )
    for ref, value in zip(refs[ways:], updated):
        ref[...] = value


def embed_adam(weight, grads, first, second, clip, rate):
    rows, width = weight.shape
    block = min(256, rows)
    state = pl.BlockSpec((block, width), lambda i: (i, 0))
    return pl.pallas_call(
        functools.partial(embed_adam_kernel, rate),
        grid=(pl.cdiv(rows, block),),
        in_specs=[pl.BlockSpec(memory_space=pltpu.SMEM)] * 2
        + [state] * 3
        + [pl.BlockSpec((grads[0].shape[0], block), lambda i: (0, i))] * len(grads),
        out_specs=[state, state, state],
        out_shape=[jax.ShapeDtypeStruct((rows, width), F32)] * 3,
        compiler_params=pltpu.CompilerParams(vmem_limit_bytes=VMEM_LIMIT),
        cost_estimate=pl.CostEstimate(
            flops=20 * rows * width, bytes_accessed=26 * rows * width, transcendentals=rows * width
        ),
        name="embed_adam",
    )(clip.reshape(1), lax.axis_index("seq").reshape(1), weight, first, second, *grads)


def token_grad_kernel(ids_ref, *refs):
    *moved_refs, head_ref, out_ref, sums_ref = refs
    block = sums_ref.shape[0]

    @pl.when(pl.program_id(1) == 0)
    def _():
        sums_ref[...] = jnp.zeros_like(sums_ref)

    first = pl.program_id(0) * block
    for batch, moved_ref in enumerate(moved_refs):
        ids = ids_ref[0, batch : batch + 1, :]
        vocab = lax.broadcasted_iota(jnp.int32, (block, ids.shape[1]), 0) + first
        chosen = jnp.where(vocab == ids, 1.0, 0.0).astype(BF16)
        moved = jnp.concatenate([moved_ref[0, way] for way in range(moved_ref.shape[1])], 1)
        sums_ref[...] += contract(chosen, moved, 1, 1)

    @pl.when(pl.program_id(1) == pl.num_programs(1) - 1)
    def _():
        out_ref[...] = (sums_ref[...].T + head_ref[...]).astype(BF16)


def token_grad(ids, moved, head_grad):
    owners, count, tokens = ids.shape
    part, vocab_rows = head_grad.shape
    block = min(1024, -(-vocab_rows // 128) * 128)
    return pl.pallas_call(
        token_grad_kernel,
        grid=(pl.cdiv(vocab_rows, block), owners),
        in_specs=[pl.BlockSpec((1, count, tokens), lambda i, j: (j, 0, 0))]
        + [pl.BlockSpec((1,) + item.shape[1:], lambda i, j: (j, 0, 0, 0)) for item in moved]
        + [pl.BlockSpec((part, block), lambda i, j: (0, i))],
        out_specs=pl.BlockSpec((part, block), lambda i, j: (0, i)),
        out_shape=jax.ShapeDtypeStruct((part, vocab_rows), BF16),
        scratch_shapes=[pltpu.VMEM((block, part), F32)],
        compiler_params=pltpu.CompilerParams(vmem_limit_bytes=VMEM_LIMIT),
        cost_estimate=pl.CostEstimate(
            flops=4 * vocab_rows * owners * count * tokens * part,
            bytes_accessed=8 * owners * count * tokens * part,
            transcendentals=0,
        ),
        name="token_grad",
    )(ids, *moved, head_grad)


def exchange(parts):
    return lax.all_to_all(parts, "seq", split_axis=0, concat_axis=0, tiled=True)


def to_relative(part, distance):
    ways = lax.axis_size("seq")
    return lax.ppermute(part, "seq", [(way, way ^ distance) for way in range(ways)])


def share(part):
    return [part] + [to_relative(part, k) for k in range(1, lax.axis_size("seq"))]


def by_source(parts):
    seq_index = lax.axis_index("seq")
    first = parts[0]
    whole = jnp.zeros(first.shape[:1] + (len(parts),) + first.shape[1:], first.dtype)
    for distance, part in enumerate(parts):
        at = (0, seq_index ^ distance) + (0,) * (first.ndim - 1)
        whole = lax.dynamic_update_slice(whole, part[:, None], at)
    return whole


def sum_of_pairs(parts):
    parts = [part.astype(F32) for part in parts]
    while len(parts) > 1:
        parts = [one + two for one, two in zip(parts[::2], parts[1::2])]
    return parts[0]


def sum_over_seq(parts):
    seq_index = lax.axis_index("seq")
    mine = lax.dynamic_index_in_dim(parts, seq_index, 0, False).astype(F32)
    for k in range(1, lax.axis_size("seq")):
        part = lax.dynamic_index_in_dim(parts, seq_index ^ k, 0, False)
        mine = mine + to_relative(part, k).astype(F32)
    return mine


def as_rows(flat):
    return jnp.pad(flat, (0, -flat.size % 1024)).reshape(-1, 128)


def sum_everywhere(parts):
    ways, owners = parts.shape[:2]
    size = parts.size // (ways * owners)
    flat = parts.reshape(ways * owners, size)
    flat = jnp.pad(flat, ((0, 0), (0, -size % 1024))).reshape(ways * owners, -1, 128)
    moved = lax.all_to_all(flat, ("seq", "fsdp"), split_axis=0, concat_axis=0, tiled=True)
    return jnp.sum(moved, 0).reshape(-1)[:size]


def after(value, *others):
    return lax.optimization_barrier((value,) + others)


def layer_forward(hidden, weights, gain_one, gain_two, router_w, tile, moe, lengths):
    dense, upward_w, downward_w = weights
    count, rows, width = hidden.shape
    output_w = dense[:, 3 * width :]
    ways = lax.axis_size("seq")
    dispatch, onehot = moe
    slots = dispatch.shape[1]
    projected, normed_one, scale_one = project(hidden, gain_one, dense, ways)
    qkv = exchange(projected)
    mixed, lse = attend(qkv, tile, lengths)
    mixed_t = exchange(mixed).reshape(width, rows)
    after_attn = hidden + contract(mixed_t, output_w, 0, 0).reshape(hidden.shape)
    normed_two, scale_two = rms_norm(after_attn, gain_two)
    normed_two = normed_two.astype(BF16)
    router_probs = jax.nn.softmax(
        matmul(normed_two.reshape(count * rows, width), router_w).reshape(count, rows, -1), -1
    )
    gate = jnp.sum(router_probs * onehot, -1, keepdims=True)
    sent = jnp.einsum("nst,ntd->nsd", dispatch, normed_two, preferred_element_type=F32).astype(BF16)
    sent = sent.reshape(count, ways, slots // ways, width).transpose(1, 0, 2, 3)
    expert_rows = exchange(sent).reshape(count * slots, width)
    upward = matmul(expert_rows, upward_w)
    activated = jax.nn.gelu(upward).astype(BF16)
    expert_out = matmul(activated, downward_w).astype(BF16)
    back = exchange(expert_out.reshape(ways, count, slots // ways, width))
    back = back.transpose(1, 0, 2, 3).reshape(count, slots, width)
    token_out = jnp.einsum("nst,nsd->ntd", dispatch, back, preferred_element_type=F32)
    result = after_attn + gate * token_out
    kept = dict(
        hidden=hidden,
        scale_one=scale_one,
        normed_one=normed_one,
        qkv=qkv,
        lse=lse,
        mixed_t=mixed_t,
        after_attn=after_attn,
        mixed=mixed,
        scale_two=scale_two,
        normed_two=normed_two,
        router_probs=router_probs,
        gate=gate,
        expert_rows=expert_rows,
        upward=upward,
        activated=activated,
        token_out=token_out,
    )
    return (result, kept)


def experts_backward(grad_out, kept, weights, moe):
    _, upward_w, downward_w = weights
    count, rows, width = grad_out.shape
    ways = lax.axis_size("seq")
    dispatch, _ = moe
    slots = dispatch.shape[1]
    grad_token = (kept["gate"] * grad_out).astype(BF16)
    sent = jnp.einsum("nst,ntd->nsd", dispatch, grad_token, preferred_element_type=F32).astype(BF16)
    sent = sent.reshape(count, ways, slots // ways, width).transpose(1, 0, 2, 3)
    grad_expert = exchange(sent).reshape(count * slots, width)
    grad_activated = contract(grad_expert, downward_w, 1, 1)
    grad_upward = jax.vjp(jax.nn.gelu, kept["upward"])[1](grad_activated)[0].astype(BF16)
    grad_rows = contract(grad_upward, upward_w, 1, 1).astype(BF16)
    back = exchange(grad_rows.reshape(ways, count, slots // ways, width))
    return (back, ((kept["expert_rows"], grad_upward), (kept["activated"], grad_expert)))


def mixed_backward(grad_out, back, kept, weights, gain_two, router_w, moe):
    dense, _, _ = weights
    count, rows, width = grad_out.shape
    output_w = dense[:, 3 * width :]
    ways = lax.axis_size("seq")
    dispatch, onehot = moe
    slots = dispatch.shape[1]
    flat = (count * rows, width)
    grad_gate = jnp.sum(grad_out * kept["token_out"], -1, keepdims=True)
    back = back.transpose(1, 0, 2, 3).reshape(count, slots, width)
    grad_normed = jnp.einsum("nst,nsd->ntd", dispatch, back, preferred_element_type=F32)
    grad_probs = onehot * grad_gate
    router_probs = kept["router_probs"]
    grad_logits = (
        router_probs * (grad_probs - jnp.sum(grad_probs * router_probs, -1, keepdims=True))
    ).astype(BF16)
    grad_logits = grad_logits.reshape(count * rows, -1)
    grad_router = contract(kept["normed_two"].reshape(flat), grad_logits, 0, 0)
    grad_normed = grad_normed.reshape(flat) + contract(grad_logits, router_w, 1, 1)
    grad_mid, grad_gain_two = rms_back(
        kept["after_attn"].reshape(flat), kept["scale_two"].reshape(-1, 1), gain_two, grad_normed
    )
    grad_mid = grad_mid + grad_out.reshape(flat)
    grad_attn = grad_mid.astype(BF16)
    grad_mixed_t = contract(output_w, grad_attn, 1, 1).astype(BF16)
    grad_mixed_t = exchange(grad_mixed_t.reshape(ways, 1, width // ways, rows))
    return (grad_mixed_t, grad_mid, (kept["mixed_t"], grad_attn), (grad_gain_two, grad_router))


def attention_backward(grad_mixed_t, grad_mid, kept, weights, gain_one, tile, lengths, piece):
    dense, _, _ = weights
    count, rows, width = kept["hidden"].shape
    attend_w = dense[:, : 3 * width]
    flat = (count * rows, width)
    grad_mixed_t, piece = after(grad_mixed_t, piece)
    grad_qkv, grad_relative = attend_back(kept["qkv"], grad_mixed_t, kept["lse"], tile, lengths)
    grad_qkv, piece = after(grad_qkv, sum_over_seq(piece))
    grad_projected_t = exchange(grad_qkv).reshape(3 * width, rows)
    grad_first, grad_gain_one = rms_back(
        kept["hidden"].reshape(flat),
        kept["scale_one"].reshape(-1, 1),
        gain_one,
        contract(grad_projected_t, attend_w, 0, 1),
    )
    return (
        (grad_mid + grad_first).reshape(count, rows, width),
        (kept["normed_one"].reshape(flat), grad_projected_t),
        (grad_gain_one, grad_relative),
        piece,
    )


def weight_grad(pairs, left_dim, right_dim):
    return contract(
        jnp.concatenate([item[0] for item in pairs], left_dim),
        jnp.concatenate([item[1] for item in pairs], right_dim),
        left_dim,
        right_dim,
    ).astype(BF16)


def adam_update(weight, grad, first, second, rate):
    first = BETA_ONE * first + (1.0 - BETA_ONE) * grad
    second = BETA_TWO * second + (1.0 - BETA_TWO) * grad * grad
    mean_hat = first / (1.0 - BETA_ONE**STEP_COUNT)
    square_hat = second / (1.0 - BETA_TWO**STEP_COUNT)
    weight = weight - rate * (
        mean_hat / (jnp.sqrt(square_hat) + ADAM_EPSILON) + WEIGHT_DECAY * weight
    )
    return (weight, first, second)


def scatter_owners(item):
    return lax.psum_scatter(item, "fsdp", scatter_dimension=0, tiled=True)


def sum_squares(*arrays):
    return sum(jnp.sum(jnp.square(item.astype(F32))) for item in arrays)


def per_device(
    token_ids,
    lengths,
    routes,
    positions,
    targets,
    teacher_index,
    teacher_weight,
    buckets,
    embed_weight,
    embed_mean,
    embed_square,
    attend_weight,
    attend_mean,
    attend_square,
    output_weight,
    output_mean,
    output_square,
    upward_weight,
    upward_mean,
    upward_square,
    downward_weight,
    downward_mean,
    downward_square,
    router_weight,
    router_mean,
    router_square,
    gains_weight,
    gains_mean,
    gains_square,
    bias_weight,
    bias_mean,
    bias_square,
):
    ways, owners = lax.axis_size("seq"), lax.axis_size("fsdp")
    seq_index, owner_index = lax.axis_index("seq"), lax.axis_index("fsdp")
    layers, experts = upward_weight.shape[0], upward_weight.shape[1]
    vocab_rows, width = embed_weight.shape
    count, rows = token_ids.shape[0], token_ids.shape[2]
    total = rows * ways
    picks = positions.shape[2]
    shard = upward_weight.shape[2]
    part = width // ways
    capacity = rows * 3 // 8
    factor = width ** (-0.5)
    lengths = lengths[:, 0]

    def dense_shard(layer):
        attend_low = attend_weight[layer].reshape(shard, 3, ways, part).transpose(0, 2, 1, 3)
        return jnp.concatenate(
            [attend_low.reshape(shard, 3 * width).astype(BF16), output_weight[layer].astype(BF16)], 1
        )

    def gather_owners(item):
        return lax.all_gather(item, "fsdp", axis=0, tiled=True)

    def gather_expert(item, layer):
        mine = lax.dynamic_index_in_dim(item[layer], seq_index, 0, False)
        return gather_owners(mine.astype(BF16))

    first_dense = dense_shard(0)
    own_ids, first_dense = after(token_ids[:, 0], first_dense)
    first_dense = gather_owners(first_dense)
    group_ids = lax.all_gather(own_ids, "fsdp", axis=0, tiled=False)
    valid_own = (seq_index * rows + positions[:, 0] < lengths[:, None]).astype(F32)
    teacher_own = teacher_weight[:, 0] / jnp.sum(teacher_weight[:, 0], -1, keepdims=True)
    small = jnp.concatenate(
        [
            lax.optimization_barrier(item.astype(BF16)).astype(F32).reshape(-1)
            for item in (gains_weight, bias_weight, router_weight)
        ]
        + [item.astype(F32).reshape(-1) for item in (valid_own, targets, teacher_index, teacher_own)]
    )
    small = lax.all_gather(as_rows(small), "fsdp", axis=0, tiled=False)
    embed_low = embed_weight.astype(BF16)
    vocab_ids = jnp.arange(vocab_rows)
    founds = []
    for batch in range(count):
        local_ids = group_ids[:, batch].reshape(-1) - owner_index * vocab_rows
        if batch == count - 1:
            local_ids, small = after(local_ids, small)
        founds.append(
            matmul((local_ids[:, None] == vocab_ids[None, :]).astype(BF16), embed_low).astype(BF16)
        )
        if batch == count - 1:
            founds[-1], first_dense = after(founds[-1], first_dense)
    later = (attend_weight, output_weight, upward_weight, downward_weight)
    founds[-1], *later = after(founds[-1], *later)
    hiddens = [
        lax.psum_scatter(
            found.reshape(owners, rows, width), "fsdp", scatter_dimension=0, tiled=False
        )
        .astype(F32)
        .reshape(1, rows, width)
        for found in founds
    ]
    weights = []
    for layer in range(layers):
        weights.append(
            (
                gather_owners(dense_shard(layer)) if layer else first_dense,
                gather_expert(later[2], layer),
                gather_expert(later[3], layer),
            )
        )

    small = small.reshape(owners, -1)
    pieces, at = [], 0
    for item in (gains_weight, bias_weight, router_weight, valid_own, targets, teacher_index, teacher_own):
        pieces.append(small[:, at : at + item.size])
        at += item.size
    norms = 2 * layers + 1
    gains_full = pieces[0].reshape(owners, norms, shard).transpose(1, 0, 2).reshape(norms, width)
    bias_full = pieces[1].reshape(owners, layers, -1).transpose(1, 0, 2).reshape(layers, -1, H)
    router_full = (
        pieces[2].reshape(owners, layers, shard, experts).transpose(1, 0, 2, 3).astype(BF16)
    ).reshape(layers, width, experts)
    valid_all = pieces[3].reshape(-1)
    targets_all = pieces[4].astype(jnp.int32).reshape(-1, 1)
    index_all = pieces[5].astype(jnp.int32).reshape(-1, teacher_index.shape[3])
    teacher_all = pieces[6].reshape(-1, teacher_index.shape[3])

    head_local = H // ways
    local_tables = lax.dynamic_slice_in_dim(bias_full, seq_index * head_local, head_local, 2)
    onehot_buckets = (buckets[:, None] == jnp.arange(bias_full.shape[1])[None, :]).astype(F32)
    tiles = [
        bias_tile(
            jnp.dot(onehot_buckets, local_tables[layer], precision=HIGHEST_PRECISION).T, rows, total
        )
        for layer in range(layers)
    ]

    route_ids = routes[:, 0, :, 0]
    onehot = (route_ids[..., None] == jnp.arange(experts)).astype(F32)
    ranks = jnp.sum((jnp.cumsum(onehot, 1) - 1.0) * onehot, -1).astype(jnp.int32)
    slot_index = route_ids * capacity + ranks
    dispatch = (slot_index[:, None, :] == jnp.arange(experts * capacity)[None, :, None]).astype(BF16)

    base = owner_index * vocab_rows
    entry = jnp.concatenate([index_all, targets_all], 1) - base
    mass = jnp.concatenate([teacher_all, jnp.ones_like(teacher_all[:, :1])], 1)
    lanes = 128
    groups = -(-vocab_rows // lanes)
    entry = jnp.where((entry >= 0) & (entry < vocab_rows), entry, groups * lanes)
    high = (entry[..., None] // lanes == jnp.arange(groups)).astype(F32) * mass[..., None]
    low = (entry[..., None] % lanes == jnp.arange(lanes)).astype(F32)
    wanted = jnp.einsum("rkh,rkl->rhl", high, low, precision=HIGHEST_PRECISION)
    wanted = wanted.reshape(-1, groups * lanes)[:, :vocab_rows]
    mass_all = jnp.sum(teacher_all, -1, keepdims=True) + 1.0

    kept_all = [[None] * count for layer in range(layers)]
    moes = [(dispatch[batch : batch + 1], onehot[batch : batch + 1]) for batch in range(count)]
    used = [lengths[batch : batch + 1] for batch in range(count)]
    for layer in range(layers):
        for batch in range(count):
            if layer == 0 and batch:
                hiddens[batch], wanted, _ = after(hiddens[batch], wanted, kept_all[0][batch - 1]["mixed"])
            hiddens[batch], kept_all[layer][batch] = layer_forward(
                hiddens[batch],
                weights[layer],
                gains_full[2 * layer],
                gains_full[2 * layer + 1],
                router_full[layer],
                tiles[layer],
                moes[batch],
                used[batch],
            )
        if layer == 0:
            every_id = lax.all_gather(group_ids, "seq", axis=0, tiled=False) - owner_index * vocab_rows
            every_id = every_id.transpose(1, 2, 0, 3).reshape(owners, count, -1)
            hiddens[-1], every_id = after(hiddens[-1], every_id)
    hidden = jnp.concatenate(hiddens, 0)

    final, scale_final = rms_norm(hidden, gains_full[2 * layers])
    chosen = (positions[:, 0][..., None] == jnp.arange(rows)).astype(BF16)
    picked = jnp.einsum("npt,ntd->npd", chosen, final.astype(BF16), preferred_element_type=F32)
    picked = lax.all_gather(
        picked.astype(BF16).reshape(count * picks, width), "fsdp", axis=0, tiled=True
    )
    logits = contract(picked, embed_low, 1, 1) * factor
    peak = jnp.max(logits, -1)
    stats = jnp.stack([peak, jnp.sum(jnp.exp(logits - peak[:, None]), -1)])
    stats = lax.all_gather(stats, "fsdp", axis=0, tiled=False)
    peak_all = jnp.max(stats[:, 0], 0)
    lse_all = peak_all + jnp.log(jnp.sum(stats[:, 1] * jnp.exp(stats[:, 0] - peak_all), 0))
    grad_logits = mass_all * jnp.exp(logits - lse_all[:, None]) - wanted
    grad_logits = (grad_logits * valid_all[:, None]).astype(BF16)
    lse_own = lax.dynamic_slice_in_dim(lse_all, owner_index * count * picks, count * picks, 0)
    mass_own = jnp.sum(teacher_own, -1) + 1.0
    own_rows = jnp.sum(teacher_own * jnp.log(teacher_own), -1) + mass_own * lse_own.reshape(count, picks)
    loss_part = jnp.sum(valid_own * own_rows) - jnp.sum(
        valid_all * jnp.sum(wanted * logits, -1)
    )
    grad_picked = lax.psum_scatter(
        matmul(grad_logits, embed_low), "fsdp", scatter_dimension=0, tiled=True
    )
    grad_picked = (grad_picked * factor).reshape(count, picks, width)
    head_grad = (matmul(lax.optimization_barrier(picked.T), grad_logits) * factor).astype(BF16)
    head_grad = head_grad.reshape(ways, part, vocab_rows)
    run = -(-vocab_rows // (128 * layers * count)) * 128
    pieces = [head_grad[:, :, at : at + run] for at in range(0, vocab_rows, run)]
    pieces += [None] * (layers * count - len(pieces))
    summed = []
    grad_final = jnp.einsum(
        "npt,npd->ntd", chosen.astype(F32), grad_picked, precision=HIGHEST_PRECISION
    )
    grad_hidden, grad_gain_final = rms_back(
        hidden.reshape(count * rows, width),
        scale_final.reshape(-1, 1),
        gains_full[2 * layers],
        grad_final.reshape(count * rows, width),
    )
    grad_hidden = grad_hidden.reshape(hidden.shape)
    grad_hiddens = [grad_hidden[batch : batch + 1] for batch in range(count)]

    gain_grads = [None] * norms
    gain_grads[2 * layers] = grad_gain_final
    router_grads, table_grads = [None] * layers, [None] * layers
    grad_parts = [None] * layers
    for layer in reversed(range(layers)):
        one, two = 2 * layer, 2 * layer + 1
        stages, passed = [None] * count, grad_parts[layer + 1] if layer + 1 < layers else None
        for batch in range(count):
            back, pairs = experts_backward(
                grad_hiddens[batch], kept_all[layer][batch], weights[layer], moes[batch]
            )
            if passed and batch < 2:
                back, passed[batch] = after(back, passed[batch])
            stages[batch] = (back, pairs)
        up_down = [
            weight_grad([pairs[which] for _, pairs in stages], 0, 0) for which in range(2)
        ]
        grad_parts[layer] = [scatter_owners(item) for item in up_down]
        outer, smalls = [], []
        for batch in range(count):
            grad_mixed_t, grad_mid, pair, small_two = mixed_backward(
                grad_hiddens[batch],
                stages[batch][0],
                kept_all[layer][batch],
                weights[layer],
                gains_full[two],
                router_full[layer],
                moes[batch],
            )
            if batch == count - 1:
                grad_mixed_t, *up_down = after(grad_mixed_t, *up_down)
                if passed:
                    grad_mixed_t, passed[2] = after(grad_mixed_t, passed[2])
                if layer == 0:
                    grad_mixed_t, grad_parts[0][0] = after(grad_mixed_t, grad_parts[0][0])
            grad_hiddens[batch], attend_pair, small_one, piece = attention_backward(
                grad_mixed_t,
                grad_mid,
                kept_all[layer][batch],
                weights[layer],
                gains_full[one],
                tiles[layer],
                used[batch],
                pieces[len(summed)],
            )
            summed.append(piece)
            outer.append((attend_pair, pair))
            smalls.append(small_one + small_two)
        gain_grads[one], grad_relative, gain_grads[two], router_grads[layer] = (
            sum(items) for items in zip(*smalls)
        )
        table_grads[layer] = jnp.dot(onehot_buckets.T, grad_relative.T, precision=HIGHEST_PRECISION)
        dense_grad = jnp.concatenate(
            [weight_grad([item[0] for item in outer], 0, 1), weight_grad([item[1] for item in outer], 1, 0)],
            1,
        )
        if layer:
            grad_hiddens[0], dense_grad = after(grad_hiddens[0], dense_grad)
            grad_parts[layer].append(scatter_owners(dense_grad))

    moved = []
    for batch in range(count):
        columns = grad_hiddens[batch].reshape(rows, width).astype(BF16).T
        moved.append(exchange(columns.reshape(ways, part, rows)))
    moved[-1], grad_parts[0][1] = after(moved[-1], grad_parts[0][1])
    up_parts = jnp.stack([parts[0] for parts in grad_parts])
    down_parts = [parts[1] for parts in grad_parts]
    dense_parts = [parts[2] for parts in grad_parts[1:]]
    moved[-1], up_parts, *dense_parts = after(moved[-1], up_parts, *dense_parts)
    moved = [lax.all_gather(item, "fsdp", axis=0, tiled=False) for item in moved]
    moved[-1], dense_grad, *down_parts = after(moved[-1], dense_grad, *down_parts)
    grad_parts[0].append(scatter_owners(dense_grad))
    head_grad = jnp.concatenate([piece for piece in summed if piece is not None], 1)
    up_whole = share(up_parts)
    down_whole = [lax.all_gather(item, "seq", axis=0, tiled=False) for item in down_parts]
    embed_part = token_grad(every_id, moved, head_grad)
    dense_sum = [sum_of_pairs(share(item)) for item in [grad_parts[0][2]] + dense_parts]
    dense_sum = jnp.stack(dense_sum)

    tables = lax.dynamic_update_slice(
        jnp.zeros(bias_full.shape, F32), jnp.stack(table_grads), (0, 0, seq_index * head_local)
    )
    bias_shard = bias_weight.shape[1]
    tiny = jnp.concatenate(
        [
            jnp.stack(gain_grads).reshape(norms, owners, shard).transpose(1, 0, 2).reshape(owners, -1),
            tables.reshape(layers, owners, bias_shard).transpose(1, 0, 2).reshape(owners, -1),
            jnp.stack(router_grads)
            .reshape(layers, owners, shard, experts)
            .transpose(1, 0, 2, 3)
            .reshape(owners, -1),
            jnp.broadcast_to(jnp.stack([loss_part, jnp.sum(valid_own)])[None], (owners, 2)),
        ],
        1,
    )
    tiny = sum_everywhere(jnp.broadcast_to(tiny[None], (ways,) + tiny.shape))
    gain_size, bias_size = gains_weight.size, bias_weight.size
    gains_grad = tiny[:gain_size].reshape(gains_weight.shape)
    bias_grad = tiny[gain_size : gain_size + bias_size].reshape(bias_weight.shape)
    router_grad = tiny[gain_size + bias_size : -2].reshape(router_weight.shape)
    loss_value, loss_count = tiny[-2], tiny[-1]

    squares_part = (
        sum_squares(embed_part, up_parts, *down_parts)
        + sum_squares(dense_sum, gains_grad, bias_grad, router_grad) / ways
    )
    grad_norm = jnp.sqrt(
        sum_everywhere(jnp.broadcast_to(squares_part, (ways, owners, 1)))[0]
    )
    clip_factor = jnp.minimum(1.0, CLIP_NORM / (grad_norm + 1e-06))

    embed_grads = share(embed_part)
    upward_grad = by_source(up_whole)
    attend_grad = dense_sum[:, :, : 3 * width].reshape(layers, shard, ways, 3, part)
    attend_grad = attend_grad.transpose(0, 1, 3, 2, 4).reshape(layers, shard, 3 * width)
    output_grad = dense_sum[:, :, 3 * width :]
    grads = (
        None,
        attend_grad,
        output_grad,
        upward_grad,
        None,
        router_grad,
        gains_grad,
        bias_grad,
    )
    params = (
        embed_weight,
        attend_weight,
        output_weight,
        upward_weight,
        downward_weight,
        router_weight,
        gains_weight,
        bias_weight,
    )
    means = (
        embed_mean,
        attend_mean,
        output_mean,
        upward_mean,
        downward_mean,
        router_mean,
        gains_mean,
        bias_mean,
    )
    squares = (
        embed_square,
        attend_square,
        output_square,
        upward_square,
        downward_square,
        router_square,
        gains_square,
        bias_square,
    )
    results = [loss_value, loss_count, grad_norm]
    states = [None] * len(params)
    states[0] = embed_adam(
        embed_weight, embed_grads, embed_mean, embed_square, clip_factor, STEP_RATES[0]
    )
    for index in (3, 4, 1, 2, 5, 6, 7):
        grad = grads[index]
        if index == 4:
            grad = jnp.stack(after(states[3][0], *down_whole)[1:])
        states[index] = adam_update(
            params[index],
            grad.astype(F32) * clip_factor,
            means[index],
            squares[index],
            STEP_RATES[index],
        )
    for state in states:
        results.extend(state)
    return tuple(results)


def solution(mesh):
    token = P(None, "fsdp", "seq")
    entry = P(None, "fsdp", "seq", None)
    state = (
        [P("fsdp", None)] * 3
        + [P(None, "fsdp", None)] * 6
        + [P(None, None, "fsdp", None)] * 6
        + [P(None, "fsdp", None)] * 3
        + [P(None, "fsdp")] * 6
    )
    return jax.shard_map(
        per_device,
        mesh=mesh,
        in_specs=tuple([token, P(None, "fsdp"), entry, token, token, entry, entry, P()] + state),
        out_specs=tuple([P(), P(), P()] + state),
        check_vma=False,
    )
```
